128 devices in a mesh: chan: 32 (over z_lo, x, y), hour: 4 (over z_hi, core).
Axes of the slice: x: 4, y: 4, z: 4 (z_hi: 2, z_lo: 2; z = z_hi * 2 + z_lo), core: 2. Of those that a mesh axis runs over, the one named last changes fastest.
Arguments:
- samples: bfloat16 [128, 1024, 1024], P('hour', 'chan'), may hold values from -400 to 400, as said below
- gap_starts: int32 [128, 4], P('hour'), may hold values from 0 to 1023
- valid_counts: int32 [128], P('hour'), may hold values from 512 to 1024
- owners: int32 [128, 1], P('hour'), may hold values from 0 to 7
- pair_mask: int32 [1024, 17, 32], P('chan'), may hold values 0 or 1
Outputs:
- xstack: bfloat16 [1024, 17, 32, 2, 512], P('chan', None, None, None, 'hour')
The draws below stay inside these ranges and needn't reach their ends.
Inputs may be any that keep to these rules, and one draw needn't show every extreme that they name: `owners`: every owner group of the window owns at least one segment. `samples`: products of a channel gain, a slowly varying envelope and noise with a part common to all channels.
All inputs are finite; a program needn't handle non-finite values. No bound on the sum of `pair_mask` on one device may be relied on, other than what follows from the above.
Results may differ from the reference program's by a relative error of at most 0.0035.
Values may be sent and summed in bfloat16 or wider, within the bound.
No kernel may reach another device: no remote copies, remote signals or barrier semaphores. Data moves between devices by JAX's collectives and lax.ppermute only.
A program may use at most 192 MiB of HBM per device.

```python
import math
import jax
import jax.numpy as jnp
from jax import lax

CH_DEV = 32
L = 1024
HGROUPS = 8
GAPS = 4
BINS = 512
GAPW = 32
RAMW = 64
SMW = 64
SEGMENTS = 128
CHANNELS = 1024
STOPS = 17
N_CHAN = 32


def draw_samples(key, part):
    key = jax.random.fold_in(key, 7)
    keys = jax.random.split(key, 4)
    gains = jnp.exp(jax.random.uniform(keys[0], (1, CHANNELS, 1), jnp.float32, 0.0, math.log(10.0)))
    envelope = jnp.exp(jax.random.uniform(keys[1], (SEGMENTS, CHANNELS, L // 16), jnp.float32, 0.0, math.log(10.0)))
    envelope = jnp.repeat(envelope, 16, axis=2)
    own_noise = jnp.clip(jax.random.normal(keys[2], (SEGMENTS, CHANNELS, L), jnp.float32), -4.0, 4.0)
    shared_noise = jnp.clip(jax.random.normal(keys[3], (SEGMENTS, 1, L), jnp.float32), -4.0, 4.0)
    share = 0.5
    return (gains * envelope * (share * shared_noise + (1.0 - share) * own_noise)).astype(jnp.bfloat16)


def touch_ends(entries, rng, least, largest):
    longest = entries.shape.index(max(entries.shape))
    spots = []
    for shift in (0, 1):
        where = [jax.random.randint(jax.random.fold_in(rng, axis), (), 0, length) for axis, length in enumerate(entries.shape)]
        where[longest] = (where[longest] + shift) % entries.shape[longest]
        spots.append(tuple(where))
    return entries.at[spots[0]].set(least).at[spots[1]].set(largest)


def distinct(key, rows, count, top, lift):
    ranking = jax.random.permutation(jax.random.fold_in(key, 1), count)
    boost = ranking
    for power in range(3):
        boost = boost * boost // count
    boost = boost * lift // count
    chance = jax.random.randint(jax.random.fold_in(key, 2), (rows, count), 0, 4096) + boost
    sure = jax.random.permutation(jax.random.fold_in(key, 3), rows)[jnp.arange(count) % rows]
    chance = jnp.where(jnp.arange(rows)[:, None] == sure[None, :], 1 << 14, chance)
    score = chance * count + jnp.arange(count)
    return lax.top_k(score.astype(jnp.int32), top)[1].astype(jnp.int32)


def setup_inputs(seed: int = 0) -> dict:
    splits = jax.random.split(jax.random.key(seed), 6)
    return {
        "samples": draw_samples(jax.random.fold_in(splits[5], 71), 0),
        "gap_starts": touch_ends(jax.random.randint(splits[1], (SEGMENTS, GAPS), 0, L), jax.random.fold_in(splits[1], 1), 0, L - 1).astype(jnp.int32),
        "valid_counts": touch_ends(jax.random.randint(splits[2], (SEGMENTS,), L // 2, L + 1), jax.random.fold_in(splits[2], 1), L // 2, L).astype(jnp.int32),
        "owners": distinct(splits[3], SEGMENTS, HGROUPS, 1, 2048),
        "pair_mask": touch_ends((jax.random.randint(splits[4], (CHANNELS, STOPS, CH_DEV), 0, 4) < 3).astype(jnp.int32), jax.random.fold_in(splits[4], 1), 0, 1),
    }


def window_mean(values, half_width):
    length = values.shape[-1]
    places = jnp.arange(length, dtype=jnp.int32)
    upper = jnp.minimum(places + half_width, length - 1)
    lower = jnp.maximum(places - half_width, 0)
    running = jnp.cumsum(values, axis=-1)
    running = jnp.concatenate([jnp.zeros(values.shape[:-1] + (1,), values.dtype), running], axis=-1)
    total = jnp.take(running, upper + 1, axis=-1) - jnp.take(running, lower, axis=-1)
    return total / (upper - lower + 1).astype(values.dtype)

def valid_samples(gap_starts, valid_counts):
    places = jnp.arange(L, dtype=jnp.int32)
    inside = places[None, :] < valid_counts[:, None]
    starts = gap_starts[:, :, None]
    holes = jnp.any((places[None, None, :] >= starts) & (places[None, None, :] < starts + GAPW), axis=1)
    return inside & jnp.logical_not(holes)

def dft_table():
    places = jnp.arange(L, dtype=jnp.int32)
    freqs = jnp.arange(BINS, dtype=jnp.int32)
    phase = places[:, None] * freqs[None, :] % L
    angle = 2.0 * math.pi / L * phase.astype(jnp.float32)
    return jnp.concatenate([jnp.cos(angle), -jnp.sin(angle)], axis=1).astype(jnp.bfloat16)

def taper_window():
    places = jnp.arange(L, dtype=jnp.int32).astype(jnp.float32)
    return 0.5 - 0.5 * jnp.cos(2.0 * math.pi / L * places)

def combine(product, width):
    leading = product.shape[:-3]
    columns = product.shape[-1]
    parts = product.reshape(leading + (width, 2, width, 2, columns))
    real_part = parts[..., :, 0, :, 0, :] + parts[..., :, 1, :, 1, :]
    imag_part = parts[..., :, 1, :, 0, :] - parts[..., :, 0, :, 1, :]
    return jnp.stack([real_part, imag_part], axis=-2).astype(jnp.bfloat16)

def reference(samples, gap_starts, valid_counts, owners, pair_mask):
    valid = valid_samples(gap_starts, valid_counts)
    masked = jnp.where(valid[:, None, :], samples, jnp.zeros((), samples.dtype))
    level = window_mean(jnp.abs(masked.astype(jnp.float32)), RAMW)
    normalized = (taper_window() * masked.astype(jnp.float32) / (level + 1e-06)).astype(jnp.bfloat16)
    spectrum = jnp.dot(normalized.reshape(SEGMENTS * CHANNELS, L).astype(jnp.float32), dft_table().astype(jnp.float32), precision=lax.Precision.HIGHEST)
    power = spectrum[:, :BINS] ** 2 + spectrum[:, BINS:] ** 2
    smooth = window_mean(power, SMW)
    member = (owners[:, 0:1] == jnp.arange(HGROUPS, dtype=jnp.int32)[None, :]).astype(jnp.float32)
    group_size = lax.optimization_barrier(jnp.sum(member, axis=0))
    weight = lax.optimization_barrier(jnp.sum(member / (HGROUPS * group_size)[None, :], axis=1))
    factor = jnp.repeat(jnp.sqrt(weight), CHANNELS)[:, None] * lax.rsqrt(smooth + 1e-06)
    whitened = (spectrum.reshape(SEGMENTS * CHANNELS, 2, BINS) * factor[:, None, :]).astype(jnp.bfloat16)
    flat = whitened.astype(jnp.float32).reshape(SEGMENTS, N_CHAN, CH_DEV * 2, BINS)

    def one_stop(stop_index):
        partner = jnp.roll(flat, -stop_index, axis=1)
        product = jnp.einsum('sgxf,sgyf->gxyf', flat, partner, precision=lax.Precision.HIGHEST)
        return combine(product, CH_DEV)
    stacks = lax.map(one_stop, jnp.arange(STOPS, dtype=jnp.int32))
    xstack = jnp.transpose(stacks, (1, 2, 0, 3, 4, 5)).reshape(CHANNELS, STOPS, CH_DEV, 2, BINS)
    return xstack * pair_mask[:, :, :, None, None].astype(jnp.bfloat16)
```

```python
import functools
import math

import jax
import jax.numpy as jnp
import ml_dtypes
import numpy as np
from jax import lax
from jax.experimental import pallas as pl
from jax.experimental.pallas import tpu as pltpu
from jax.sharding import Mesh, PartitionSpec as P

L = 1024
HGROUPS = 8
BINS = 512
GAPW = 32
RAMW = 64
SMW = 64
NF = 8
PARTS = 4
MB = 1024 * 1024


def band_np(length, half_width):
    places = np.arange(length)
    return (np.abs(places[:, None] - places[None, :]) <= half_width).astype(ml_dtypes.bfloat16)


def inverse_count_np(length, half_width):
    places = np.arange(length)
    upper = np.minimum(places + half_width, length - 1)
    lower = np.maximum(places - half_width, 0)
    return (1.0 / (upper - lower + 1)).astype(np.float32)


def dft_rows_np():
    phase = np.arange(BINS)[:, None] * np.arange(L)[None, :] % L
    angle = 2.0 * math.pi / L * phase
    return np.concatenate([np.cos(angle), -np.sin(angle)], axis=0).astype(ml_dtypes.bfloat16)


def taper_np():
    return (0.5 - 0.5 * np.cos(2.0 * math.pi / L * np.arange(L))).astype(np.float32)


def spread_np():
    table = np.zeros((256, 512), np.float32)
    c = np.arange(128)
    table[c, 2 * c] = 1
    table[128 + c, 2 * c + 1] = -1
    table[128 + c, 256 + 2 * c] = 1
    table[c, 256 + 2 * c + 1] = 1
    return table.astype(ml_dtypes.bfloat16)


def dot(a, b, contract=((1,), (0,))):
    return lax.dot_general(a, b, (contract, ((), ())), preferred_element_type=jnp.float32)


def lanes(shape):
    return lax.broadcasted_iota(jnp.int32, shape, len(shape) - 1)


WROWS = 256


def whiten_kernel(x_ref, valid_ref, root_ref, band_ref, taper_ref, icount_ref, dft_ref, bband_ref, bcount_ref, out_ref, held):
    step = pl.program_id(0)
    x = x_ref[...].astype(jnp.float32).reshape(WROWS // 32, 32, L) * valid_ref[...][:, None, :]
    x = x.reshape(WROWS, L)
    level = dot(jnp.abs(x).astype(jnp.bfloat16), band_ref[...]) * icount_ref[...]
    normalized = (taper_ref[...] * x / (level + 1e-06)).astype(jnp.bfloat16)
    spectrum = dot(dft_ref[...], normalized, ((1,), (1,)))
    real, imag = spectrum[:BINS], spectrum[BINS:]
    power = real * real + imag * imag
    high = power.astype(jnp.bfloat16)
    low = (power - high.astype(jnp.float32)).astype(jnp.bfloat16)
    smooth = (dot(bband_ref[...], high) + dot(bband_ref[...], low)) * bcount_ref[...]
    factor = lax.rsqrt(smooth + 1e-06) * root_ref[...]
    real, imag = real * factor, imag * factor
    first = lanes((BINS, 128)) < 64
    for tile in range(WROWS // 128):
        re = real[:, tile * 128 : (tile + 1) * 128]
        im = imag[:, tile * 128 : (tile + 1) * 128]
        at = step * (WROWS // 64) + tile * 2
        held[pl.ds(at, 1)] = jnp.where(first, re, pltpu.roll(im, 64, 1))[None]
        held[pl.ds(at + 1, 1)] = jnp.where(first, pltpu.roll(re, 64, 1), im)[None]

    @pl.when(step == pl.num_programs(0) - 1)
    def _():
        for block in range(BINS // 64):
            part = held[:, block * 64 : (block + 1) * 64, :]
            out_ref[block * 64 : (block + 1) * 64] = jnp.swapaxes(part, 0, 1).astype(jnp.bfloat16)


def whiten(rows, valid, root):
    whole = lambda *shape: pl.BlockSpec(shape, lambda i: (0,) * len(shape))
    return pl.pallas_call(
        whiten_kernel,
        grid=(1024 // WROWS,),
        in_specs=[
            pl.BlockSpec((WROWS, L), lambda i: (i, 0)),
            pl.BlockSpec((WROWS // 32, L), lambda i: (i, 0)),
            pl.BlockSpec((1, WROWS), lambda i: (0, i)),
            whole(L, L),
            whole(1, L),
            whole(1, L),
            whole(2 * BINS, L),
            whole(BINS, BINS),
            whole(BINS, 1),
        ],
        out_specs=whole(BINS, 16, 128),
        out_shape=jax.ShapeDtypeStruct((BINS, 16, 128), jnp.bfloat16),
        scratch_shapes=[pltpu.VMEM((16, BINS, 128), jnp.float32)],
        compiler_params=pltpu.CompilerParams(vmem_limit_bytes=48 * MB),
        name="whiten",
    )(
        rows,
        valid,
        root,
        jnp.asarray(band_np(L, RAMW)),
        jnp.asarray(taper_np()[None, :]),
        jnp.asarray(inverse_count_np(L, RAMW)[None, :]),
        jnp.asarray(dft_rows_np()),
        jnp.asarray(band_np(BINS, SMW)),
        jnp.asarray(inverse_count_np(BINS, SMW)[:, None]),
    )


def assemble_kernel(piece_ref, out_ref):
    count = piece_ref.shape[1]
    pieces = []
    for y in range(4):
        both = [piece_ref[h * 4 + y].astype(jnp.float32) for h in range(4)]
        pieces.append(jnp.stack(both, axis=1).reshape(count * 64, 128))
    group = lanes((count * 64, 128)) // 32
    for part in range(2):
        for bit in range(2):
            block = part * 2 + bit
            total = None
            for y in range(4):
                shift = (32 * (y - block)) % 128
                moved = pieces[y] if shift == 0 else pltpu.roll(pieces[y], shift, 1)
                total = moved if total is None else jnp.where(group == y, moved, total)
            out_ref[:, bit * 64 : (bit + 1) * 64, part * 128 : (part + 1) * 128] = total.reshape(
                count, 64, 128
            ).astype(jnp.bfloat16)


def assemble(pieces):
    bins = pieces.shape[1]
    return pl.pallas_call(
        assemble_kernel,
        grid=(bins // NF,),
        in_specs=[pl.BlockSpec((16, NF, 16, 128), lambda i: (0, i, 0, 0))],
        out_specs=pl.BlockSpec((NF, 128, 256), lambda i: (i, 0, 0)),
        out_shape=jax.ShapeDtypeStruct((bins, 128, 256), jnp.bfloat16),
        compiler_params=pltpu.CompilerParams(vmem_limit_bytes=32 * MB),
        name="assemble",
    )(pieces)


ROWS = 34 * NF


def cross_kernel(y_ref, own_ref, v1_ref, v2_ref, v3_ref, v4_ref, spread_ref, *rest):
    outs, (held, zero_stop) = rest[:4], rest[4:]
    y = y_ref[0]
    group = lanes((32, 256)) // 64
    first = lanes((32, 128)) < 64
    for f in range(NF):
        own = own_ref[f]
        left = jnp.concatenate([own[:, :128].T, own[:, 128:].T], axis=1)
        products = []
        for visitor in (own_ref, v1_ref, v2_ref, v3_ref, v4_ref):
            wide = dot(visitor[f], spread_ref[...]).astype(jnp.bfloat16)
            right = jnp.concatenate([wide[:, :256], wide[:, 256:]], axis=0)
            products.append(dot(left, right))
        for m in range(1, 4):
            held[f, :, m * 256 : (m + 1) * 256] = products[m]
        for g in range(4):
            at = slice(g * 32, (g + 1) * 32)
            held[f, at, :256] = jnp.where(group <= g, products[4][at], products[0][at])
            tile = products[0][at, (g // 2) * 128 : (g // 2 + 1) * 128]
            turned = pltpu.roll(tile, 64, 1)
            zero_stop[f, at, :] = jnp.where(first, tile, turned) if g % 2 == 0 else jnp.where(first, turned, tile)
    pair = lanes((16, NF, 128)) < 64
    for s in range(4):
        g = lax.rem(y + s, 4)
        for i in range(0, 32, 8):
            rows = held[:, pl.ds(pl.multiple_of(g * 32 + i, 8), 8), :]
            outs[s][i * NF : (i + 8) * NF, :] = (
                jnp.swapaxes(rows, 0, 1).reshape(8 * NF, 1024).astype(jnp.bfloat16)
            )
        rows = zero_stop[:, pl.ds(pl.multiple_of(g * 32, 32), 32), :]
        rows = jnp.swapaxes(rows, 0, 1).reshape(16, 2, NF, 128)
        rows = jnp.where(pair, rows[:, 0], rows[:, 1]).astype(jnp.float32)
        for u in range(8):
            both = jnp.concatenate([rows[u], rows[8 + u]], axis=0)
            outs[s][32 * NF :, u * 128 : (u + 1) * 128] = both.astype(jnp.bfloat16)


def cross(y, part, own, visitors):
    block = lambda: pl.BlockSpec((NF, 128, 256), lambda i, y: (0, 0, 0))
    out = lambda: pl.BlockSpec((ROWS, 1024), lambda i, y: (0, 0))
    return pl.pallas_call(
        cross_kernel,
        grid_spec=pltpu.PrefetchScalarGridSpec(
            num_scalar_prefetch=1,
            grid=(1,),
            in_specs=[
                pl.BlockSpec((NF, 128, 256), lambda i, y: (part, 0, 0)),
                block(),
                block(),
                block(),
                block(),
                pl.BlockSpec((256, 512), lambda i, y: (0, 0)),
            ],
            out_specs=[out() for _ in range(4)],
            scratch_shapes=[
                pltpu.VMEM((NF, 128, 1024), jnp.float32),
                pltpu.VMEM((NF, 128, 128), jnp.float32),
            ],
        ),
        out_shape=[jax.ShapeDtypeStruct((ROWS, 1024), jnp.bfloat16)] * 4,
        compiler_params=pltpu.CompilerParams(vmem_limit_bytes=40 * MB),
        name="cross",
    )(y, own, *visitors, jnp.asarray(spread_np()))


def finish_kernel(y_ref, mask_ref, mask0_ref, *rest):
    pieces, ends, out_ref, held, held0, turned = rest[:16], rest[16:32], rest[32], rest[33], rest[34], rest[35]
    step = pl.program_id(0)
    y = y_ref[0]

    def row(index):
        source = lax.rem(y + 4 - index % 4, 4)
        return pl.multiple_of(source * 32 + (index // 4) * NF, 8)

    @pl.when(step == 0)
    def _():
        for index in range(16):
            both = ends[index][...].astype(jnp.float32)
            held0[pl.ds(row(index), NF), :1024] = both[:NF]
            held0[pl.ds(row(index), NF), 1024:] = both[NF:]

    for index in range(16):
        both = pieces[index][...].astype(jnp.float32)
        held[0, pl.ds(row(index), NF), :] = both[:NF]
        held[1, pl.ds(row(index), NF), :] = both[NF:]
    zero = held0[:, pl.ds(pl.multiple_of(step * 128, 128), 128)] * mask0_ref[0]
    zero = zero.T.astype(jnp.bfloat16)
    for i in range(2):
        out_ref[i * 1088 : i * 1088 + 64, :] = zero[i * 64 : (i + 1) * 64]
        for tile in range(8):
            at = slice(tile * 128, (tile + 1) * 128)
            block = (held[i, :, at] * mask_ref[0, i : i + 1, at]).T.astype(jnp.bfloat16)
            for half in range(2):
                stop = lax.rem(tile * 2 + half + 15 - y, 16) + 1
                out_ref[pl.ds(pl.multiple_of(i * 1088 + stop * 64, 64), 64), :] = block[half * 64 : (half + 1) * 64]


def finish(y, mask, mask0, pieces):
    return pl.pallas_call(
        finish_kernel,
        grid_spec=pltpu.PrefetchScalarGridSpec(
            num_scalar_prefetch=1,
            grid=(16,),
            in_specs=[
                pl.BlockSpec((1, 2, 1024), lambda i, y: (i, 0, 0)),
                pl.BlockSpec((1, 1, 128), lambda i, y: (i, 0, 0)),
            ]
            + [pl.BlockSpec((2 * NF, 1024), lambda i, y: (i, 0)) for _ in range(16)]
            + [pl.BlockSpec((2 * NF, 1024), lambda i, y: (16, 0)) for _ in range(16)],
            out_specs=pl.BlockSpec((2 * 1088, 128), lambda i, y: (i, 0)),
            scratch_shapes=[
                pltpu.VMEM((2, 128, 1024), jnp.float32),
                pltpu.VMEM((128, 2048), jnp.float32),
                pltpu.VMEM((8, 128), jnp.float32),
            ],
        ),
        out_shape=jax.ShapeDtypeStruct((34816, 128), jnp.bfloat16),
        compiler_params=pltpu.CompilerParams(vmem_limit_bytes=40 * MB),
        name="finish",
    )(y, mask, mask0, *pieces, *pieces)


def hour_sum(value):
    total = value
    for zh, core in ((0, 1), (1, 0), (1, 1)):
        route = [(i, i ^ (zh * 2 + core)) for i in range(4)]
        total = total + lax.ppermute(value, ("zh", "core"), route)
    return total


def body(samples, gap_starts, valid_counts, owners, pair_mask):
    places = jnp.arange(L, dtype=jnp.int32)
    inside = places[None, :] < valid_counts[:, None]
    starts = gap_starts[:, :, None]
    holes = jnp.any((places[None, None, :] >= starts) & (places[None, None, :] < starts + GAPW), axis=1)
    valid = (inside & jnp.logical_not(holes)).astype(jnp.float32)
    member = (owners == jnp.arange(HGROUPS, dtype=jnp.int32)[None, :]).astype(jnp.float32)
    group_size = hour_sum(jnp.sum(member, axis=0))
    weight = jnp.sum(member / (HGROUPS * group_size)[None, :], axis=1)
    root = jnp.repeat(jnp.sqrt(weight), 32)[None, :]

    y = lax.axis_index("y").astype(jnp.int32)
    y_arg = y[None]
    mask = jnp.repeat(pair_mask.astype(jnp.float32), 2, axis=2)
    mask0 = mask[:, 0].reshape(16, 1, 128)
    mask = jnp.roll(mask[:, 1:], y + 1, axis=1).reshape(16, 2, 1024)

    spectra = whiten(samples.reshape(1024, L), valid, root)
    pieces = lax.all_to_all(spectra, ("zh", "core", "y"), 0, 0, tiled=True)
    blocks = assemble(pieces.reshape(16, 32, 16, 128))

    parts = [[None] * 4 for _ in range(PARTS)]
    for part in range(PARTS):
        own = blocks[part * NF : (part + 1) * NF]
        visitors = []
        for d in range(1, 5):
            route = [(i, (i - d) % 8) for i in range(8)]
            visitors.append(lax.ppermute(own, ("zl", "x"), route))
        sent = cross(y_arg, part, blocks, visitors)
        parts[part][0] = sent[0]
        for s in range(1, 4):
            parts[part][s] = lax.ppermute(sent[s], "y", [(i, (i + s) % 4) for i in range(4)])
    flat = [parts[part][s] for part in range(PARTS) for s in range(4)]
    return finish(y_arg, mask, mask0, flat).reshape(32, 17, 32, 2, 128)


def solution(mesh):
    fine = Mesh(mesh.devices.reshape(2, 4, 4, 2, 2), ("zl", "x", "y", "zh", "core"))
    chan, hour = ("zl", "x", "y"), ("zh", "core")
    placed = (
        P(hour, chan, None),
        P(hour, None),
        P(hour),
        P(hour, None),
        P(chan, None, None),
    )
    return jax.shard_map(
        body,
        mesh=fine,
        in_specs=placed,
        out_specs=P(chan, None, None, None, hour),
        check_vma=False,
    )
```

```python
import functools
import math

import jax
import jax.numpy as jnp
import ml_dtypes
import numpy as np
from jax import lax
from jax.experimental import pallas as pl
from jax.experimental.pallas import tpu as pltpu
from jax.sharding import Mesh, PartitionSpec as P

L = 1024
HGROUPS = 8
BINS = 512
GAPW = 32
RAMW = 64
SMW = 64
NF = 8
PARTS = 4
MB = 1024 * 1024


def band_np(length, half_width):
    places = np.arange(length)
    return (np.abs(places[:, None] - places[None, :]) <= half_width).astype(ml_dtypes.bfloat16)


def inverse_count_np(length, half_width):
    places = np.arange(length)
    upper = np.minimum(places + half_width, length - 1)
    lower = np.maximum(places - half_width, 0)
    return (1.0 / (upper - lower + 1)).astype(np.float32)


def dft_rows_np():
    phase = np.arange(BINS)[:, None] * np.arange(L)[None, :] % L
    angle = 2.0 * math.pi / L * phase
    return np.concatenate([np.cos(angle), -np.sin(angle)], axis=0).astype(ml_dtypes.bfloat16)


def taper_np():
    return (0.5 - 0.5 * np.cos(2.0 * math.pi / L * np.arange(L))).astype(np.float32)


def spread_np():
    table = np.zeros((256, 512), np.float32)
    c = np.arange(128)
    table[c, 2 * c] = 1
    table[128 + c, 2 * c + 1] = -1
    table[128 + c, 256 + 2 * c] = 1
    table[c, 256 + 2 * c + 1] = 1
    return table.astype(ml_dtypes.bfloat16)


def cost(us):
    return pl.CostEstimate(flops=int(us * 1.15e9), bytes_accessed=int(us * 3.6e6), transcendentals=0)


def dot(a, b, contract=((1,), (0,))):
    return lax.dot_general(a, b, (contract, ((), ())), preferred_element_type=jnp.float32)


def lanes(shape):
    return lax.broadcasted_iota(jnp.int32, shape, len(shape) - 1)


WROWS = 256


def whiten_kernel(x_ref, valid_ref, root_ref, band_ref, taper_ref, icount_ref, dft_ref, bband_ref, bcount_ref, out_ref, held):
    step = pl.program_id(0)
    x = x_ref[...].astype(jnp.float32).reshape(WROWS // 32, 32, L) * valid_ref[...][:, None, :]
    x = x.reshape(WROWS, L)
    level = dot(jnp.abs(x).astype(jnp.bfloat16), band_ref[...]) * icount_ref[...]
    normalized = (taper_ref[...] * x / (level + 1e-06)).astype(jnp.bfloat16)
    spectrum = dot(dft_ref[...], normalized, ((1,), (1,)))
    real, imag = spectrum[:BINS], spectrum[BINS:]
    power = real * real + imag * imag
    high = power.astype(jnp.bfloat16)
    low = (power - high.astype(jnp.float32)).astype(jnp.bfloat16)
    smooth = (dot(bband_ref[...], high) + dot(bband_ref[...], low)) * bcount_ref[...]
    factor = lax.rsqrt(smooth + 1e-06) * root_ref[...]
    real, imag = real * factor, imag * factor
    first = lanes((BINS, 128)) < 64
    for tile in range(WROWS // 128):
        re = real[:, tile * 128 : (tile + 1) * 128]
        im = imag[:, tile * 128 : (tile + 1) * 128]
        at = step * (WROWS // 64) + tile * 2
        held[pl.ds(at, 1)] = jnp.where(first, re, pltpu.roll(im, 64, 1))[None]
        held[pl.ds(at + 1, 1)] = jnp.where(first, pltpu.roll(re, 64, 1), im)[None]

    @pl.when(step == pl.num_programs(0) - 1)
    def _():
        for block in range(BINS // 64):
            part = held[:, block * 64 : (block + 1) * 64, :]
            out_ref[block * 64 : (block + 1) * 64] = jnp.swapaxes(part, 0, 1).astype(jnp.bfloat16)


def whiten(rows, valid, root):
    whole = lambda *shape: pl.BlockSpec(shape, lambda i: (0,) * len(shape))
    return pl.pallas_call(
        whiten_kernel,
        grid=(1024 // WROWS,),
        in_specs=[
            pl.BlockSpec((WROWS, L), lambda i: (i, 0)),
            pl.BlockSpec((WROWS // 32, L), lambda i: (i, 0)),
            pl.BlockSpec((1, WROWS), lambda i: (0, i)),
            whole(L, L),
            whole(1, L),
            whole(1, L),
            whole(2 * BINS, L),
            whole(BINS, BINS),
            whole(BINS, 1),
        ],
        out_specs=whole(BINS, 16, 128),
        out_shape=jax.ShapeDtypeStruct((BINS, 16, 128), jnp.bfloat16),
        scratch_shapes=[pltpu.VMEM((16, BINS, 128), jnp.float32)],
        compiler_params=pltpu.CompilerParams(vmem_limit_bytes=48 * MB),
        cost_estimate=cost(12.0),
        name="whiten",
    )(
        rows,
        valid,
        root,
        jnp.asarray(band_np(L, RAMW)),
        jnp.asarray(taper_np()[None, :]),
        jnp.asarray(inverse_count_np(L, RAMW)[None, :]),
        jnp.asarray(dft_rows_np()),
        jnp.asarray(band_np(BINS, SMW)),
        jnp.asarray(inverse_count_np(BINS, SMW)[:, None]),
    )


def assemble_kernel(piece_ref, out_ref):
    count = piece_ref.shape[1]
    pieces = []
    for y in range(4):
        both = [piece_ref[h * 4 + y].astype(jnp.float32) for h in range(4)]
        pieces.append(jnp.stack(both, axis=1).reshape(count * 64, 128))
    group = lanes((count * 64, 128)) // 32
    for part in range(2):
        for bit in range(2):
            block = part * 2 + bit
            total = None
            for y in range(4):
                shift = (32 * (y - block)) % 128
                moved = pieces[y] if shift == 0 else pltpu.roll(pieces[y], shift, 1)
                total = moved if total is None else jnp.where(group == y, moved, total)
            out_ref[:, bit * 64 : (bit + 1) * 64, part * 128 : (part + 1) * 128] = total.reshape(
                count, 64, 128
            ).astype(jnp.bfloat16)


def assemble(pieces, part):
    return pl.pallas_call(
        assemble_kernel,
        grid=(1,),
        in_specs=[pl.BlockSpec((16, NF, 16, 128), lambda i: (0, part, 0, 0))],
        out_specs=pl.BlockSpec((NF, 128, 256), lambda i: (0, 0, 0)),
        out_shape=jax.ShapeDtypeStruct((NF, 128, 256), jnp.bfloat16),
        compiler_params=pltpu.CompilerParams(vmem_limit_bytes=32 * MB),
        cost_estimate=cost(0.8),
        name="assemble",
    )(pieces)


def own_side(own):
    return jnp.concatenate([own[:, :128].T, own[:, 128:].T], axis=1)


def visiting_side(block, spread):
    wide = dot(block, spread).astype(jnp.bfloat16)
    return jnp.concatenate([wide[:, :256], wide[:, 256:]], axis=0)


def put_rows(held, out, columns, g, bins):
    for i in range(0, 32, 8):
        rows = held[:, pl.ds(pl.multiple_of(g * 32 + i, 8), 8), :]
        rows = jnp.swapaxes(rows, 0, 1).reshape(8 * bins, columns)
        out[i * bins : (i + 8) * bins, :] = rows.astype(jnp.bfloat16)


def outer_kernel(y_ref, *rest):
    owns, others, spread_ref = rest[:2], rest[2:4], rest[4]
    outs, (held, zero_stop) = rest[5:9], rest[9:]
    y = y_ref[0]
    group = lanes((32, 256)) // 64
    first = lanes((32, 128)) < 64
    for f in range(2 * NF):
        own, other = owns[f // NF][f % NF], others[f // NF][f % NF]
        left = own_side(own)
        near = dot(left, visiting_side(own, spread_ref[...]))
        far = dot(left, visiting_side(other, spread_ref[...]))
        for g in range(4):
            at = slice(g * 32, (g + 1) * 32)
            held[f, at, :] = jnp.where(group <= g, far[at], near[at])
            tile = near[at, (g // 2) * 128 : (g // 2 + 1) * 128]
            turned = pltpu.roll(tile, 64, 1)
            zero_stop[f, at, :] = jnp.where(first, tile, turned) if g % 2 == 0 else jnp.where(first, turned, tile)
    pair = lanes((16, 2 * NF, 128)) < 64
    for s in range(4):
        g = lax.rem(y + s, 4)
        put_rows(held, outs[s], 256, g, 2 * NF)
        rows = zero_stop[:, pl.ds(pl.multiple_of(g * 32, 32), 32), :]
        rows = jnp.swapaxes(rows, 0, 1).reshape(16, 2, 2 * NF, 128)
        rows = jnp.where(pair, rows[:, 0], rows[:, 1]).reshape(32 * NF, 128)
        outs[s][64 * NF :, :128] = rows[: 16 * NF].astype(jnp.bfloat16)
        outs[s][64 * NF :, 128:] = rows[16 * NF :].astype(jnp.bfloat16)


def outer(y, owns, others):
    block = lambda: pl.BlockSpec((NF, 128, 256), lambda i, y: (0, 0, 0))
    return pl.pallas_call(
        outer_kernel,
        grid_spec=pltpu.PrefetchScalarGridSpec(
            num_scalar_prefetch=1,
            grid=(1,),
            in_specs=[block() for _ in range(4)] + [pl.BlockSpec((256, 512), lambda i, y: (0, 0))],
            out_specs=[pl.BlockSpec((80 * NF, 256), lambda i, y: (0, 0)) for _ in range(4)],
            scratch_shapes=[
                pltpu.VMEM((2 * NF, 128, 256), jnp.float32),
                pltpu.VMEM((2 * NF, 128, 128), jnp.float32),
            ],
        ),
        out_shape=[jax.ShapeDtypeStruct((80 * NF, 256), jnp.bfloat16)] * 4,
        compiler_params=pltpu.CompilerParams(vmem_limit_bytes=40 * MB),
        cost_estimate=cost(6.5),
        name="outer",
    )(y, *owns, *others, jnp.asarray(spread_np()))


def inner_kernel(y_ref, own_ref, v1_ref, v2_ref, v3_ref, spread_ref, *rest):
    outs, held = rest[:4], rest[4]
    y = y_ref[0]
    for f in range(NF):
        left = own_side(own_ref[f])
        for m, visitor in enumerate((v1_ref, v2_ref, v3_ref)):
            held[f, :, m * 256 : (m + 1) * 256] = dot(left, visiting_side(visitor[f], spread_ref[...]))
    for s in range(4):
        put_rows(held, outs[s], 768, lax.rem(y + s, 4), NF)


def inner(y, own, visitors):
    block = lambda: pl.BlockSpec((NF, 128, 256), lambda i, y: (0, 0, 0))
    return pl.pallas_call(
        inner_kernel,
        grid_spec=pltpu.PrefetchScalarGridSpec(
            num_scalar_prefetch=1,
            grid=(1,),
            in_specs=[block() for _ in range(4)] + [pl.BlockSpec((256, 512), lambda i, y: (0, 0))],
            out_specs=[pl.BlockSpec((32 * NF, 768), lambda i, y: (0, 0)) for _ in range(4)],
            scratch_shapes=[pltpu.VMEM((NF, 128, 768), jnp.float32)],
        ),
        out_shape=[jax.ShapeDtypeStruct((32 * NF, 768), jnp.bfloat16)] * 4,
        compiler_params=pltpu.CompilerParams(vmem_limit_bytes=40 * MB),
        cost_estimate=cost(5.5),
        name="inner",
    )(y, own, *visitors, jnp.asarray(spread_np()))


STEP = 4


def finish_kernel(y_ref, mask_ref, mask0_ref, *rest):
    outers, zeros, inners, out_ref, held, held0 = rest[:8], rest[8:16], rest[16:32], rest[32], rest[33], rest[34]
    step = pl.program_id(0)
    y = y_ref[0]

    def row(index, bins):
        source = lax.rem(y + 4 - index % 4, 4)
        return pl.multiple_of(source * 32 + (index // 4) * bins, 8)

    lane_at = pl.multiple_of(step // 4 * 128, 128)
    for index in range(8):
        bins = 2 * NF
        both = outers[index][...].astype(jnp.float32)
        for i in range(STEP):
            held[i, pl.ds(row(index, bins), bins), :256] = both[i * bins : (i + 1) * bins]
        both = zeros[index][:, pl.ds(lane_at, 128)].astype(jnp.float32)
        for pair in range(2):
            held0[pair, pl.ds(row(index, bins), bins), :] = both[pair * bins : (pair + 1) * bins]
    for index in range(16):
        both = inners[index][...].astype(jnp.float32)
        for i in range(STEP):
            held[i, pl.ds(row(index, NF), NF), 256:] = both[i * NF : (i + 1) * NF]
    for i in range(STEP):
        if i % 2 == 0:
            zero = (held0[i // 2] * mask0_ref[i // 2]).T.astype(jnp.bfloat16)
        out_ref[i * 1088 : i * 1088 + 64, :] = zero[i % 2 * 64 : (i % 2 + 1) * 64]
        for tile in range(8):
            at = slice(tile * 128, (tile + 1) * 128)
            block = (held[i, :, at] * mask_ref[0, i : i + 1, at]).T.astype(jnp.bfloat16)
            for half in range(2):
                stop = lax.rem(tile * 2 + half + 15 - y, 16) + 1
                out_ref[pl.ds(pl.multiple_of(i * 1088 + stop * 64, 64), 64), :] = block[half * 64 : (half + 1) * 64]


def finish(y, mask, mask0, outers, inners):
    return pl.pallas_call(
        finish_kernel,
        grid_spec=pltpu.PrefetchScalarGridSpec(
            num_scalar_prefetch=1,
            grid=(32 // STEP,),
            in_specs=[
                pl.BlockSpec((1, STEP, 1024), lambda i, y: (i, 0, 0)),
                pl.BlockSpec((STEP // 2, 1, 128), lambda i, y: (i, 0, 0)),
            ]
            + [pl.BlockSpec((STEP * 2 * NF, 256), lambda i, y: (i, 0)) for _ in range(8)]
            + [pl.BlockSpec((STEP * NF, 256), lambda i, y: (16 + i % 4, 0)) for _ in range(8)]
            + [pl.BlockSpec((STEP * NF, 768), lambda i, y: (i, 0)) for _ in range(16)],
            out_specs=pl.BlockSpec((STEP * 1088, 128), lambda i, y: (i, 0)),
            scratch_shapes=[
                pltpu.VMEM((STEP, 128, 1024), jnp.float32),
                pltpu.VMEM((STEP // 2, 128, 128), jnp.float32),
            ],
        ),
        out_shape=jax.ShapeDtypeStruct((34816, 128), jnp.bfloat16),
        compiler_params=pltpu.CompilerParams(vmem_limit_bytes=40 * MB),
        cost_estimate=cost(9.0),
        name="finish",
    )(y, mask, mask0, *outers, *outers, *inners)


def shift(block, axis, distance):
    size = lax.axis_size(axis)
    return lax.ppermute(block, axis, [(i, (i + distance) % size) for i in range(size)])


def tie(block, after):
    return block if after is None else lax.optimization_barrier((block, after))[0]


def hour_sum(value):
    total = value
    for zh, core in ((0, 1), (1, 0), (1, 1)):
        route = [(i, i ^ (zh * 2 + core)) for i in range(4)]
        total = total + lax.ppermute(value, ("zh", "core"), route)
    return total


def body(samples, gap_starts, valid_counts, owners, pair_mask):
    places = jnp.arange(L, dtype=jnp.int32)
    inside = places[None, :] < valid_counts[:, None]
    starts = gap_starts[:, :, None]
    holes = jnp.any((places[None, None, :] >= starts) & (places[None, None, :] < starts + GAPW), axis=1)
    valid = (inside & jnp.logical_not(holes)).astype(jnp.float32)
    member = (owners == jnp.arange(HGROUPS, dtype=jnp.int32)[None, :]).astype(jnp.float32)
    group_size = hour_sum(jnp.sum(member, axis=0))
    weight = jnp.sum(member / (HGROUPS * group_size)[None, :], axis=1)
    root = jnp.repeat(jnp.sqrt(weight), 32)[None, :]

    y = lax.axis_index("y").astype(jnp.int32)
    y_arg = y[None]
    mask = jnp.repeat(pair_mask.astype(jnp.float32), 2, axis=2)
    mask0 = mask[:, 0].reshape(16, 1, 128)
    mask = jnp.roll(mask[:, 1:], y + 1, axis=1).reshape(32 // STEP, STEP, 1024)

    spectra = whiten(samples.reshape(1024, L), valid, root)
    pieces = lax.all_to_all(spectra, ("zh", "core", "y"), 0, 0, tiled=True)
    pieces = pieces.reshape(16, 32, 16, 128)
    owns = [assemble(pieces, part) for part in range(PARTS)]

    x = lax.axis_index("x")

    def gather(part, after):
        send = lambda d, after: shift(tie(jnp.where(x < d, swapped[part], owns[part]), after), "x", -d)
        one, three = send(1, after), send(3, after)
        return one, send(2, (one, three)), three

    def send_back(sent):
        return (sent[0], shift(sent[1], "y", 1), shift(sent[2], "y", 2), shift(sent[3], "y", 3))

    def do_outer(half, after):
        pair = slice(2 * half, 2 * half + 2)
        first, *others = owns[pair]
        return send_back(outer(y_arg, [tie(first, after), *others], swapped[pair]))

    def do_inner(part, visitors, after):
        return send_back(inner(y_arg, tie(owns[part], after), visitors))

    swapped = []
    for part in range(PARTS):
        swapped.append(shift(tie(owns[part], swapped[part - 2] if part >= 2 else None), "zl", 1))
    v0 = gather(0, None)
    a0 = do_outer(0, v0[0])
    v1 = gather(1, (v0[0], v0[2], a0[0]))
    b0 = do_inner(0, v0, (a0[1], a0[3]))
    a1 = do_outer(1, (a0[2], b0[0]))
    v2 = gather(2, (v1[0], v1[2], b0[0]))
    b1 = do_inner(1, v1, (b0[1], b0[3], a1[0]))
    v3 = gather(3, (v2[0], v2[2], b1[0]))
    b2 = do_inner(2, v2, (b0[2], *a1))
    b3 = do_inner(3, v3, (*b1, b2[0]))
    outers, inners = (a0, a1), (b0, b1, b2, b3)
    flat_outer = [outers[half][s] for half in range(2) for s in range(4)]
    flat_inner = [inners[part][s] for part in range(PARTS) for s in range(4)]
    return finish(y_arg, mask, mask0, flat_outer, flat_inner).reshape(32, 17, 32, 2, 128)


def solution(mesh):
    fine = Mesh(mesh.devices.reshape(2, 4, 4, 2, 2), ("zl", "x", "y", "zh", "core"))
    chan, hour = ("zl", "x", "y"), ("zh", "core")
    placed = (
        P(hour, chan, None),
        P(hour, None),
        P(hour),
        P(hour, None),
        P(chan, None, None),
    )
    return jax.shard_map(
        body,
        mesh=fine,
        in_specs=placed,
        out_specs=P(chan, None, None, None, hour),
        check_vma=False,
    )
```

```python
import functools
import math

import jax
import jax.numpy as jnp
import ml_dtypes
import numpy as np
from jax import lax
from jax.experimental import pallas as pl
from jax.experimental.pallas import tpu as pltpu
from jax.sharding import Mesh, PartitionSpec as P

L = 1024
HGROUPS = 8
BINS = 512
GAPW = 32
RAMW = 64
SMW = 64
NF = 8
PARTS = 4
MB = 1024 * 1024


def band_np(length, half_width):
    places = np.arange(length)
    return (np.abs(places[:, None] - places[None, :]) <= half_width).astype(ml_dtypes.bfloat16)


def inverse_count_np(length, half_width):
    places = np.arange(length)
    upper = np.minimum(places + half_width, length - 1)
    lower = np.maximum(places - half_width, 0)
    return (1.0 / (upper - lower + 1)).astype(np.float32)


def dft_rows_np():
    phase = np.arange(BINS)[:, None] * np.arange(L)[None, :] % L
    angle = 2.0 * math.pi / L * phase
    return np.concatenate([np.cos(angle), -np.sin(angle)], axis=0).astype(ml_dtypes.bfloat16)


def taper_np():
    return (0.5 - 0.5 * np.cos(2.0 * math.pi / L * np.arange(L))).astype(np.float32)


def spread_np():
    table = np.zeros((256, 512), np.float32)
    c = np.arange(128)
    table[c, 2 * c] = 1
    table[128 + c, 2 * c + 1] = -1
    table[128 + c, 256 + 2 * c] = 1
    table[c, 256 + 2 * c + 1] = 1
    return table.astype(ml_dtypes.bfloat16)


def cost(us):
    return pl.CostEstimate(flops=int(us * 3.45e+10), bytes_accessed=int(us * 1.08e+08), transcendentals=0)


def dot(a, b, contract=((1,), (0,))):
    return lax.dot_general(a, b, (contract, ((), ())), preferred_element_type=jnp.float32)


def lanes(shape):
    return lax.broadcasted_iota(jnp.int32, shape, len(shape) - 1)


WROWS = 256


def level_kernel(x_ref, valid_ref, band_ref, taper_ref, icount_ref, out_ref):
    x = x_ref[...].astype(jnp.float32).reshape(WROWS // 32, 32, L) * valid_ref[...][:, None, :]
    x = x.reshape(WROWS, L)
    level = dot(jnp.abs(x).astype(jnp.bfloat16), band_ref[...]) * icount_ref[...]
    out_ref[...] = (taper_ref[...] * x / (level + 1e-06)).astype(jnp.bfloat16)


def whole(*shape):
    return pl.BlockSpec(shape, lambda *i: (0,) * len(shape))


def normalize(rows, valid):
    return pl.pallas_call(
        level_kernel,
        grid=(1024 // WROWS,),
        in_specs=[
            pl.BlockSpec((WROWS, L), lambda i: (i, 0)),
            pl.BlockSpec((WROWS // 32, L), lambda i: (i, 0)),
            whole(L, L),
            whole(1, L),
            whole(1, L),
        ],
        out_specs=pl.BlockSpec((WROWS, L), lambda i: (i, 0)),
        out_shape=jax.ShapeDtypeStruct((1024, L), jnp.bfloat16),
        compiler_params=pltpu.CompilerParams(vmem_limit_bytes=48 * MB),
        cost_estimate=cost(6.0),
        name="normalize",
    )(
        rows,
        valid,
        jnp.asarray(band_np(L, RAMW)),
        jnp.asarray(taper_np()[None, :]),
        jnp.asarray(inverse_count_np(L, RAMW)[None, :]),
    )


def whiten_kernel(x_ref, root_ref, dft_ref, bband_ref, bcount_ref, out0, out1, out23, held):
    step = pl.program_id(0)
    spectrum = dot(dft_ref[...], x_ref[...], ((1,), (1,)))
    real, imag = spectrum[:BINS], spectrum[BINS:]
    power = real * real + imag * imag
    high = power.astype(jnp.bfloat16)
    low = (power - high.astype(jnp.float32)).astype(jnp.bfloat16)
    smooth = (dot(bband_ref[...], high) + dot(bband_ref[...], low)) * bcount_ref[...]
    factor = lax.rsqrt(smooth + 1e-06) * root_ref[...]
    real, imag = real * factor, imag * factor
    first = lanes((BINS, 128)) < 64
    for tile in range(WROWS // 128):
        re = real[:, tile * 128 : (tile + 1) * 128]
        im = imag[:, tile * 128 : (tile + 1) * 128]
        at = step * (WROWS // 64) + tile * 2
        held[pl.ds(at, 1)] = jnp.where(first, re, pltpu.roll(im, 64, 1))[None]
        held[pl.ds(at + 1, 1)] = jnp.where(first, pltpu.roll(re, 64, 1), im)[None]

    @pl.when(step == pl.num_programs(0) - 1)
    def _():
        for block in range(BINS // 64):
            part = held[:, block * 64 : (block + 1) * 64, :]
            part = jnp.swapaxes(part, 0, 1).astype(jnp.bfloat16).reshape(2, 32, 16, 128)
            out0[block * 2 : block * 2 + 2] = part[:, :NF]
            out1[block * 2 : block * 2 + 2] = part[:, NF : 2 * NF]
            out23[block * 2 : block * 2 + 2] = part[:, 2 * NF :]


def whiten(rows, root):
    return pl.pallas_call(
        whiten_kernel,
        grid=(1024 // WROWS,),
        in_specs=[
            pl.BlockSpec((WROWS, L), lambda i: (i, 0)),
            pl.BlockSpec((1, WROWS), lambda i: (0, i)),
            whole(2 * BINS, L),
            whole(BINS, BINS),
            whole(BINS, 1),
        ],
        out_specs=[whole(16, NF, 16, 128), whole(16, NF, 16, 128), whole(16, 2 * NF, 16, 128)],
        out_shape=[
            jax.ShapeDtypeStruct((16, NF, 16, 128), jnp.bfloat16),
            jax.ShapeDtypeStruct((16, NF, 16, 128), jnp.bfloat16),
            jax.ShapeDtypeStruct((16, 2 * NF, 16, 128), jnp.bfloat16),
        ],
        scratch_shapes=[pltpu.VMEM((16, BINS, 128), jnp.float32)],
        compiler_params=pltpu.CompilerParams(vmem_limit_bytes=48 * MB),
        cost_estimate=cost(9.0),
        name="whiten",
    )(
        rows,
        root,
        jnp.asarray(dft_rows_np()),
        jnp.asarray(band_np(BINS, SMW)),
        jnp.asarray(inverse_count_np(BINS, SMW)[:, None]),
    )


def assemble_kernel(piece_ref, out_ref):
    count = piece_ref.shape[1]
    pieces = []
    for y in range(4):
        both = [piece_ref[h * 4 + y].astype(jnp.float32) for h in range(4)]
        pieces.append(jnp.stack(both, axis=1).reshape(count * 64, 128))
    group = lanes((count * 64, 128)) // 32
    for part in range(2):
        for bit in range(2):
            block = part * 2 + bit
            total = None
            for y in range(4):
                shift = (32 * (y - block)) % 128
                moved = pieces[y] if shift == 0 else pltpu.roll(pieces[y], shift, 1)
                total = moved if total is None else jnp.where(group == y, moved, total)
            out_ref[:, bit * 64 : (bit + 1) * 64, part * 128 : (part + 1) * 128] = total.reshape(
                count, 64, 128
            ).astype(jnp.bfloat16)


def assemble(pieces, part):
    return pl.pallas_call(
        assemble_kernel,
        grid=(1,),
        in_specs=[pl.BlockSpec((16, NF, 16, 128), lambda i: (0, part, 0, 0))],
        out_specs=whole(NF, 128, 256),
        out_shape=jax.ShapeDtypeStruct((NF, 128, 256), jnp.bfloat16),
        compiler_params=pltpu.CompilerParams(vmem_limit_bytes=32 * MB),
        cost_estimate=cost(0.8),
        name="assemble",
    )(pieces)


def own_side(own):
    return jnp.concatenate([own[:, :128].T, own[:, 128:].T], axis=1)


def visiting_side(block, spread):
    wide = dot(block, spread).astype(jnp.bfloat16)
    return jnp.concatenate([wide[:, :256], wide[:, 256:]], axis=0)


def cross_kernel(own_ref, v1_ref, v2_ref, v3_ref, v4_ref, spread_ref, out, held, zero_stop):
    group = lanes((32, 256)) // 64
    first = lanes((32, 128)) < 64
    for f in range(NF):
        own = own_ref[f]
        left = own_side(own)
        near = dot(left, visiting_side(own, spread_ref[...]))
        far = dot(left, visiting_side(v4_ref[f], spread_ref[...]))
        for m, visitor in enumerate((v1_ref, v2_ref, v3_ref)):
            held[f, :, (m + 1) * 256 : (m + 2) * 256] = dot(left, visiting_side(visitor[f], spread_ref[...]))
        for g in range(4):
            at = slice(g * 32, (g + 1) * 32)
            held[f, at, :256] = jnp.where(group <= g, far[at], near[at])
            tile = near[at, (g // 2) * 128 : (g // 2 + 1) * 128]
            turned = pltpu.roll(tile, 64, 1)
            zero_stop[f, at, :] = jnp.where(first, tile, turned) if g % 2 == 0 else jnp.where(first, turned, tile)
    pair = lanes((16, NF, 128)) < 64
    for g in range(4):
        for i in range(0, 32, 8):
            rows = jnp.swapaxes(held[:, g * 32 + i : g * 32 + i + 8, :], 0, 1)
            out[g, i * NF : (i + 8) * NF, :] = rows.reshape(8 * NF, 1024).astype(jnp.bfloat16)
        rows = jnp.swapaxes(zero_stop[:, g * 32 : (g + 1) * 32, :], 0, 1).reshape(16, 2, NF, 128)
        rows = jnp.where(pair, rows[:, 0], rows[:, 1])
        for u in range(8):
            both = jnp.concatenate([rows[2 * u], rows[2 * u + 1]], axis=0)
            out[g, 32 * NF :, u * 128 : (u + 1) * 128] = both.astype(jnp.bfloat16)


def cross(own, visitors):
    return pl.pallas_call(
        cross_kernel,
        grid=(1,),
        in_specs=[whole(NF, 128, 256) for _ in range(5)] + [whole(256, 512)],
        out_specs=whole(4, 34 * NF, 1024),
        scratch_shapes=[
            pltpu.VMEM((NF, 128, 1024), jnp.float32),
            pltpu.VMEM((NF, 128, 128), jnp.float32),
        ],
        out_shape=jax.ShapeDtypeStruct((4, 34 * NF, 1024), jnp.bfloat16),
        compiler_params=pltpu.CompilerParams(vmem_limit_bytes=60 * MB),
        cost_estimate=cost(10.0),
        name="cross",
    )(own, *visitors, jnp.asarray(spread_np()))


STEP = 4


def finish_kernel(y_ref, mask_ref, mask0_ref, *rest):
    pieces, zeros, (out_ref, held, held0) = rest[:PARTS], rest[PARTS : 2 * PARTS], rest[2 * PARTS :]
    step = pl.program_id(0)
    y = y_ref[0]
    lane_at = pl.multiple_of(step * 128, 128)
    for source in range(4):
        for part in range(PARTS):
            row = slice(source * 32 + part * NF, source * 32 + (part + 1) * NF)
            both = pieces[part][source].astype(jnp.float32)
            for i in range(STEP):
                held[i, row, :] = both[i * NF : (i + 1) * NF]
            both = zeros[part][source, :, pl.ds(lane_at, 128)].astype(jnp.float32)
            for pair in range(2):
                held0[pair, row, :] = both[pair * NF : (pair + 1) * NF]
    for i in range(STEP):
        if i % 2 == 0:
            zero = (held0[i // 2] * mask0_ref[i // 2]).T.astype(jnp.bfloat16)
        out_ref[i * 1088 : i * 1088 + 64, :] = zero[i % 2 * 64 : (i % 2 + 1) * 64]
        for tile in range(8):
            at = slice(tile * 128, (tile + 1) * 128)
            block = (held[i, :, at] * mask_ref[0, i : i + 1, at]).T.astype(jnp.bfloat16)
            for half in range(2):
                stop = lax.rem(tile * 2 + half + 15 - y, 16) + 1
                out_ref[pl.ds(pl.multiple_of(i * 1088 + stop * 64, 64), 64), :] = block[half * 64 : (half + 1) * 64]


def finish(y, mask, mask0, pieces):
    return pl.pallas_call(
        finish_kernel,
        grid_spec=pltpu.PrefetchScalarGridSpec(
            num_scalar_prefetch=1,
            grid=(32 // STEP,),
            in_specs=[
                pl.BlockSpec((1, STEP, 1024), lambda i, y: (i, 0, 0)),
                pl.BlockSpec((STEP // 2, 1, 128), lambda i, y: (i, 0, 0)),
            ]
            + [pl.BlockSpec((4, STEP * NF, 1024), lambda i, y: (0, i, 0)) for _ in range(PARTS)]
            + [pl.BlockSpec((4, 2 * NF, 1024), lambda i, y: (0, 16, 0)) for _ in range(PARTS)],
            out_specs=pl.BlockSpec((STEP * 1088, 128), lambda i, y: (i, 0)),
            scratch_shapes=[
                pltpu.VMEM((STEP, 128, 1024), jnp.float32),
                pltpu.VMEM((STEP // 2, 128, 128), jnp.float32),
            ],
        ),
        out_shape=jax.ShapeDtypeStruct((34816, 128), jnp.bfloat16),
        compiler_params=pltpu.CompilerParams(vmem_limit_bytes=60 * MB),
        cost_estimate=cost(9.0),
        name="finish",
    )(y, mask, mask0, *pieces, *pieces)


def shift(block, axis, distance):
    size = lax.axis_size(axis)
    return lax.ppermute(block, axis, [(i, (i + distance) % size) for i in range(size)])


def tie(block, after):
    return block if after is None else lax.optimization_barrier((block, after))[0]


def hour_sum(value):
    total = value
    for zh, core in ((0, 1), (1, 0), (1, 1)):
        route = [(i, i ^ (zh * 2 + core)) for i in range(4)]
        total = total + lax.ppermute(value, ("zh", "core"), route)
    return total


def body(samples, gap_starts, valid_counts, owners, pair_mask):
    places = jnp.arange(L, dtype=jnp.int32)
    inside = places[None, :] < valid_counts[:, None]
    starts = gap_starts[:, :, None]
    holes = jnp.any((places[None, None, :] >= starts) & (places[None, None, :] < starts + GAPW), axis=1)
    valid = (inside & jnp.logical_not(holes)).astype(jnp.float32)
    member = (owners == jnp.arange(HGROUPS, dtype=jnp.int32)[None, :]).astype(jnp.float32)
    group_size = hour_sum(jnp.sum(member, axis=0))
    weight = jnp.sum(member / (HGROUPS * group_size)[None, :], axis=1)
    root = jnp.repeat(jnp.sqrt(weight), 32)[None, :]

    y = lax.axis_index("y").astype(jnp.int32)
    y_arg = y[None]
    mask = jnp.repeat(pair_mask.astype(jnp.float32), 2, axis=2)
    mask0 = mask[:, 0].reshape(16, 1, 128)
    mask = jnp.roll(mask[:, 1:], y + 1, axis=1).reshape(32 // STEP, STEP, 1024)

    spectra = whiten(normalize(samples.reshape(1024, L), valid), root)

    def transpose(block, after, name):
        with jax.named_scope(name):
            return lax.all_to_all(tie(block, after), ("zh", "core", "y"), 0, 0, tiled=True)

    def swap(part):
        with jax.named_scope(f"z{part}"):
            return shift(owns[part], "zl", 1)

    p0 = transpose(spectra[0], None, "p0")
    p1 = transpose(spectra[1], p0, "p1")
    p23 = transpose(spectra[2], p1, "p23")
    owns = [assemble(p0, 0)]
    swapped = [swap(0)]
    owns.append(assemble(tie(p1, swapped[0]), 0))
    swapped.append(swap(1))
    owns += [assemble(p23, 0), assemble(p23, 1)]
    swapped += [swap(2), swap(3)]

    x = lax.axis_index("x")

    def exchange(block, name):
        with jax.named_scope(name):
            return lax.all_to_all(block, "y", 0, 0, tiled=True)

    def gather(part, d, after):
        with jax.named_scope(f"x{part}_{d}"):
            return shift(tie(jnp.where(x < d, swapped[part], owns[part]), after), "x", -d)

    def do_cross(part, visitors, after):
        return cross(tie(owns[part], after), (*visitors, swapped[part]))

    def gather_all(part, before, last):
        return [gather(part, 1, before), gather(part, 2, last), gather(part, 3, before)]

    v0 = gather_all(0, None, None)
    c0 = do_cross(0, v0, None)
    y0 = exchange(tie(c0, p23), "y0")
    v1 = gather_all(1, None, v0)
    c1 = do_cross(1, v1, c0)
    y1 = exchange(tie(c1, y0), "y1")
    v2 = gather_all(2, v0, v1)
    c2 = do_cross(2, v2, (c1, y0))
    y2 = exchange(tie(c2, y1), "y2")
    v3 = gather_all(3, v1, v2)
    c3 = do_cross(3, v3, (c2, y1))
    y3 = exchange(tie(c3, y2), "y3")
    return finish(y_arg, mask, mask0, (y0, y1, y2, y3)).reshape(32, 17, 32, 2, 128)


def solution(mesh):
    fine = Mesh(mesh.devices.reshape(2, 4, 4, 2, 2), ("zl", "x", "y", "zh", "core"))
    chan, hour = ("zl", "x", "y"), ("zh", "core")
    placed = (
        P(hour, chan, None),
        P(hour, None),
        P(hour),
        P(hour, None),
        P(chan, None, None),
    )
    return jax.shard_map(
        body,
        mesh=fine,
        in_specs=placed,
        out_specs=P(chan, None, None, None, hour),
        check_vma=False,
    )
```

```python
import functools
import math

import jax
import jax.numpy as jnp
import ml_dtypes
import numpy as np
from jax import lax
from jax.experimental import pallas as pl
from jax.experimental.pallas import tpu as pltpu
from jax.sharding import Mesh, PartitionSpec as P

L = 1024
HGROUPS = 8
BINS = 512
GAPW = 32
RAMW = 64
SMW = 64
NF = 8
PARTS = 4
MB = 1024 * 1024


def band_np(length, half_width):
    places = np.arange(length)
    return (np.abs(places[:, None] - places[None, :]) <= half_width).astype(ml_dtypes.bfloat16)


def inverse_count_np(length, half_width):
    places = np.arange(length)
    upper = np.minimum(places + half_width, length - 1)
    lower = np.maximum(places - half_width, 0)
    return (1.0 / (upper - lower + 1)).astype(np.float32)


def dft_rows_np():
    phase = np.arange(BINS)[:, None] * np.arange(L)[None, :] % L
    angle = 2.0 * math.pi / L * phase
    return np.concatenate([np.cos(angle), -np.sin(angle)], axis=0).astype(ml_dtypes.bfloat16)


def taper_np():
    return (0.5 - 0.5 * np.cos(2.0 * math.pi / L * np.arange(L))).astype(np.float32)


def spread_np():
    table = np.zeros((256, 512), np.float32)
    c = np.arange(128)
    table[c, 2 * c] = 1
    table[128 + c, 2 * c + 1] = -1
    table[128 + c, 256 + 2 * c] = 1
    table[c, 256 + 2 * c + 1] = 1
    return table.astype(ml_dtypes.bfloat16)


def cost(us):
    return pl.CostEstimate(flops=int(us * 3.45e+10), bytes_accessed=int(us * 1.08e+08), transcendentals=0)


def dot(a, b, contract=((1,), (0,))):
    return lax.dot_general(a, b, (contract, ((), ())), preferred_element_type=jnp.float32)


def lanes(shape):
    return lax.broadcasted_iota(jnp.int32, shape, len(shape) - 1)


WROWS = 512


def level_kernel(x_ref, valid_ref, band_ref, taper_ref, icount_ref, out_ref):
    x = x_ref[...].astype(jnp.float32).reshape(WROWS // 32, 32, L) * valid_ref[...][:, None, :]
    x = x.reshape(WROWS, L)
    level = dot(jnp.abs(x).astype(jnp.bfloat16), band_ref[...]) * icount_ref[...]
    out_ref[...] = (taper_ref[...] * x / (level + 1e-06)).astype(jnp.bfloat16)


def whole(*shape):
    return pl.BlockSpec(shape, lambda *i: (0,) * len(shape))


def normalize(rows, valid):
    return pl.pallas_call(
        level_kernel,
        grid=(1024 // WROWS,),
        in_specs=[
            pl.BlockSpec((WROWS, L), lambda i: (i, 0)),
            pl.BlockSpec((WROWS // 32, L), lambda i: (i, 0)),
            whole(L, L),
            whole(1, L),
            whole(1, L),
        ],
        out_specs=pl.BlockSpec((WROWS, L), lambda i: (i, 0)),
        out_shape=jax.ShapeDtypeStruct((1024, L), jnp.bfloat16),
        compiler_params=pltpu.CompilerParams(vmem_limit_bytes=48 * MB),
        cost_estimate=cost(6.0),
        name="normalize",
    )(
        rows,
        valid,
        jnp.asarray(band_np(L, RAMW)),
        jnp.asarray(taper_np()[None, :]),
        jnp.asarray(inverse_count_np(L, RAMW)[None, :]),
    )


def whiten_kernel(x_ref, root_ref, dft_ref, bband_ref, bcount_ref, out0, out1, out23, held):
    step = pl.program_id(0)
    spectrum = dot(dft_ref[...], x_ref[...], ((1,), (1,)))
    real, imag = spectrum[:BINS], spectrum[BINS:]
    power = real * real + imag * imag
    high = power.astype(jnp.bfloat16)
    low = (power - high.astype(jnp.float32)).astype(jnp.bfloat16)
    smooth = (dot(bband_ref[...], high) + dot(bband_ref[...], low)) * bcount_ref[...]
    factor = lax.rsqrt(smooth + 1e-06) * root_ref[...]
    real, imag = real * factor, imag * factor
    first = lanes((BINS, 128)) < 64
    for tile in range(WROWS // 128):
        re = real[:, tile * 128 : (tile + 1) * 128]
        im = imag[:, tile * 128 : (tile + 1) * 128]
        at = step * (WROWS // 64) + tile * 2
        held[pl.ds(at, 1)] = jnp.where(first, re, pltpu.roll(im, 64, 1))[None]
        held[pl.ds(at + 1, 1)] = jnp.where(first, pltpu.roll(re, 64, 1), im)[None]

    @pl.when(step == pl.num_programs(0) - 1)
    def _():
        for block in range(BINS // 64):
            part = held[:, block * 64 : (block + 1) * 64, :]
            part = jnp.swapaxes(part, 0, 1).astype(jnp.bfloat16).reshape(2, 32, 16, 128)
            out0[block * 2 : block * 2 + 2] = part[:, :NF]
            out1[block * 2 : block * 2 + 2] = part[:, NF : 2 * NF]
            out23[block * 2 : block * 2 + 2] = part[:, 2 * NF :]


def whiten(rows, root):
    return pl.pallas_call(
        whiten_kernel,
        grid=(1024 // WROWS,),
        in_specs=[
            pl.BlockSpec((WROWS, L), lambda i: (i, 0)),
            pl.BlockSpec((1, WROWS), lambda i: (0, i)),
            whole(2 * BINS, L),
            whole(BINS, BINS),
            whole(BINS, 1),
        ],
        out_specs=[whole(16, NF, 16, 128), whole(16, NF, 16, 128), whole(16, 2 * NF, 16, 128)],
        out_shape=[
            jax.ShapeDtypeStruct((16, NF, 16, 128), jnp.bfloat16),
            jax.ShapeDtypeStruct((16, NF, 16, 128), jnp.bfloat16),
            jax.ShapeDtypeStruct((16, 2 * NF, 16, 128), jnp.bfloat16),
        ],
        scratch_shapes=[pltpu.VMEM((16, BINS, 128), jnp.float32)],
        compiler_params=pltpu.CompilerParams(vmem_limit_bytes=48 * MB),
        cost_estimate=cost(9.0),
        name="whiten",
    )(
        rows,
        root,
        jnp.asarray(dft_rows_np()),
        jnp.asarray(band_np(BINS, SMW)),
        jnp.asarray(inverse_count_np(BINS, SMW)[:, None]),
    )


def assemble_kernel(piece_ref, out_ref):
    count = piece_ref.shape[1]
    pieces = []
    for y in range(4):
        both = [piece_ref[h * 4 + y].astype(jnp.float32) for h in range(4)]
        pieces.append(jnp.stack(both, axis=1).reshape(count * 64, 128))
    group = lanes((count * 64, 128)) // 32
    for part in range(2):
        for bit in range(2):
            block = part * 2 + bit
            total = None
            for y in range(4):
                shift = (32 * (y - block)) % 128
                moved = pieces[y] if shift == 0 else pltpu.roll(pieces[y], shift, 1)
                total = moved if total is None else jnp.where(group == y, moved, total)
            out_ref[:, bit * 64 : (bit + 1) * 64, part * 128 : (part + 1) * 128] = total.reshape(
                count, 64, 128
            ).astype(jnp.bfloat16)


def assemble(pieces, part):
    return pl.pallas_call(
        assemble_kernel,
        grid=(1,),
        in_specs=[pl.BlockSpec((16, NF, 16, 128), lambda i: (0, part, 0, 0))],
        out_specs=whole(NF, 128, 256),
        out_shape=jax.ShapeDtypeStruct((NF, 128, 256), jnp.bfloat16),
        compiler_params=pltpu.CompilerParams(vmem_limit_bytes=32 * MB),
        cost_estimate=cost(0.8),
        name="assemble",
    )(pieces)


def own_side(own):
    return jnp.concatenate([own[:, :128].T, own[:, 128:].T], axis=1)


def visiting_side(block, spread):
    wide = dot(block, spread).astype(jnp.bfloat16)
    return jnp.concatenate([wide[:, :256], wide[:, 256:]], axis=0)


def cross_kernel(own_ref, v1_ref, v2_ref, v3_ref, v4_ref, spread_ref, out, held, zero_stop, wide):
    group = lanes((32, 256)) // 64
    first = lanes((32, 128)) < 64
    for d, visitor in enumerate((own_ref, v1_ref, v2_ref, v3_ref, v4_ref)):
        wide[d] = dot(visitor[...].reshape(NF * 128, 256), spread_ref[...]).astype(jnp.bfloat16)

    def right(d, f):
        rows = wide[d, f * 128 : (f + 1) * 128]
        return jnp.concatenate([rows[:, :256], rows[:, 256:]], axis=0)

    for f in range(NF):
        left = own_side(own_ref[f])
        near = dot(left, right(0, f))
        far = dot(left, right(4, f))
        for m in range(1, 4):
            held[f, :, m * 256 : (m + 1) * 256] = dot(left, right(m, f))
        for g in range(4):
            at = slice(g * 32, (g + 1) * 32)
            held[f, at, :256] = jnp.where(group <= g, far[at], near[at])
            tile = near[at, (g // 2) * 128 : (g // 2 + 1) * 128]
            turned = pltpu.roll(tile, 64, 1)
            zero_stop[f, at, :] = jnp.where(first, tile, turned) if g % 2 == 0 else jnp.where(first, turned, tile)
    pair = lanes((16, NF, 128)) < 64
    for g in range(4):
        for i in range(0, 32, 8):
            rows = jnp.swapaxes(held[:, g * 32 + i : g * 32 + i + 8, :], 0, 1)
            out[g, i * NF : (i + 8) * NF, :] = rows.reshape(8 * NF, 1024).astype(jnp.bfloat16)
        rows = jnp.swapaxes(zero_stop[:, g * 32 : (g + 1) * 32, :], 0, 1).reshape(16, 2, NF, 128)
        rows = jnp.where(pair, rows[:, 0], rows[:, 1])
        for u in range(8):
            both = jnp.concatenate([rows[2 * u], rows[2 * u + 1]], axis=0)
            out[g, 32 * NF :, u * 128 : (u + 1) * 128] = both.astype(jnp.bfloat16)


def cross(own, visitors):
    return pl.pallas_call(
        cross_kernel,
        grid=(1,),
        in_specs=[whole(NF, 128, 256) for _ in range(5)] + [whole(256, 512)],
        out_specs=whole(4, 34 * NF, 1024),
        scratch_shapes=[
            pltpu.VMEM((NF, 128, 1024), jnp.float32),
            pltpu.VMEM((NF, 128, 128), jnp.float32),
            pltpu.VMEM((5, NF * 128, 512), jnp.bfloat16),
        ],
        out_shape=jax.ShapeDtypeStruct((4, 34 * NF, 1024), jnp.bfloat16),
        compiler_params=pltpu.CompilerParams(vmem_limit_bytes=60 * MB),
        cost_estimate=cost(10.0),
        name="cross",
    )(own, *visitors, jnp.asarray(spread_np()))


def outer_kernel(own_ref, v4_ref, spread_ref, out, held, zero_stop, wide):
    group = lanes((32, 256)) // 64
    first = lanes((32, 128)) < 64
    for d, visitor in enumerate((own_ref, v4_ref)):
        wide[d] = dot(visitor[...].reshape(NF * 128, 256), spread_ref[...]).astype(jnp.bfloat16)

    def right(d, f):
        rows = wide[d, f * 128 : (f + 1) * 128]
        return jnp.concatenate([rows[:, :256], rows[:, 256:]], axis=0)

    for f in range(NF):
        left = own_side(own_ref[f])
        near = dot(left, right(0, f))
        far = dot(left, right(1, f))
        for g in range(4):
            at = slice(g * 32, (g + 1) * 32)
            held[f, at, :] = jnp.where(group <= g, far[at], near[at])
            tile = near[at, (g // 2) * 128 : (g // 2 + 1) * 128]
            turned = pltpu.roll(tile, 64, 1)
            zero_stop[f, at, :] = jnp.where(first, tile, turned) if g % 2 == 0 else jnp.where(first, turned, tile)
    pair = lanes((16, NF, 128)) < 64
    for g in range(4):
        for i in range(0, 32, 8):
            rows = jnp.swapaxes(held[:, g * 32 + i : g * 32 + i + 8, :], 0, 1)
            out[g, i * NF : (i + 8) * NF, :] = rows.reshape(8 * NF, 256).astype(jnp.bfloat16)
        rows = jnp.swapaxes(zero_stop[:, g * 32 : (g + 1) * 32, :], 0, 1).reshape(16, 2, NF, 128)
        rows = jnp.where(pair, rows[:, 0], rows[:, 1]).reshape(16 * NF, 128)
        out[g, 32 * NF :, :128] = rows[: 8 * NF].astype(jnp.bfloat16)
        out[g, 32 * NF :, 128:] = rows[8 * NF :].astype(jnp.bfloat16)


def inner_kernel(own_ref, v1_ref, v2_ref, v3_ref, spread_ref, out, held, wide):
    for d, visitor in enumerate((v1_ref, v2_ref, v3_ref)):
        wide[d] = dot(visitor[...].reshape(NF * 128, 256), spread_ref[...]).astype(jnp.bfloat16)
    for f in range(NF):
        left = own_side(own_ref[f])
        for m in range(3):
            rows = wide[m, f * 128 : (f + 1) * 128]
            right = jnp.concatenate([rows[:, :256], rows[:, 256:]], axis=0)
            held[f, :, m * 256 : (m + 1) * 256] = dot(left, right)
    for g in range(4):
        for i in range(0, 32, 8):
            rows = jnp.swapaxes(held[:, g * 32 + i : g * 32 + i + 8, :], 0, 1)
            out[g, i * NF : (i + 8) * NF, :] = rows.reshape(8 * NF, 768).astype(jnp.bfloat16)


def early(kernel, name, us, shape, scratch, *blocks):
    return pl.pallas_call(
        kernel,
        grid=(1,),
        in_specs=[whole(NF, 128, 256) for _ in blocks] + [whole(256, 512)],
        out_specs=whole(*shape),
        scratch_shapes=scratch,
        out_shape=jax.ShapeDtypeStruct(shape, jnp.bfloat16),
        compiler_params=pltpu.CompilerParams(vmem_limit_bytes=60 * MB),
        cost_estimate=cost(us),
        name=name,
    )(*blocks, jnp.asarray(spread_np()))


def outer(own, opposite):
    scratch = [
        pltpu.VMEM((NF, 128, 256), jnp.float32),
        pltpu.VMEM((NF, 128, 128), jnp.float32),
        pltpu.VMEM((2, NF * 128, 512), jnp.bfloat16),
    ]
    return early(outer_kernel, "outer", 3.0, (4, 40 * NF, 256), scratch, own, opposite)


def inner(own, visitors):
    scratch = [
        pltpu.VMEM((NF, 128, 768), jnp.float32),
        pltpu.VMEM((3, NF * 128, 512), jnp.bfloat16),
    ]
    return early(inner_kernel, "inner", 5.0, (4, 32 * NF, 768), scratch, own, *visitors)


STEP = 4


def finish_kernel(y_ref, mask_ref, mask0_ref, outer_ref, outer0_ref, inner_ref, *rest):
    pieces, zeros, (out_ref, held, held0) = rest[: PARTS - 1], rest[PARTS - 1 : 2 * PARTS - 2], rest[2 * PARTS - 2 :]
    step = pl.program_id(0)
    y = y_ref[0]
    lane_at = pl.multiple_of(step * 128, 128)
    first_at = pl.multiple_of(step // 4 * 128, 128)
    for source in range(4):
        row = slice(source * 32, source * 32 + NF)
        both = outer_ref[source].astype(jnp.float32)
        others = inner_ref[source].astype(jnp.float32)
        for i in range(STEP):
            held[i, row, :256] = both[i * NF : (i + 1) * NF]
            held[i, row, 256:] = others[i * NF : (i + 1) * NF]
        both = outer0_ref[source, :, pl.ds(first_at, 128)].astype(jnp.float32)
        for pair in range(2):
            held0[pair, row, :] = both[pair * NF : (pair + 1) * NF]
        for part in range(1, PARTS):
            row = slice(source * 32 + part * NF, source * 32 + (part + 1) * NF)
            both = pieces[part - 1][source].astype(jnp.float32)
            for i in range(STEP):
                held[i, row, :] = both[i * NF : (i + 1) * NF]
            both = zeros[part - 1][source, :, pl.ds(lane_at, 128)].astype(jnp.float32)
            for pair in range(2):
                held0[pair, row, :] = both[pair * NF : (pair + 1) * NF]
    for i in range(STEP):
        if i % 2 == 0:
            zero = (held0[i // 2] * mask0_ref[i // 2]).T.astype(jnp.bfloat16)
        out_ref[i * 1088 : i * 1088 + 64, :] = zero[i % 2 * 64 : (i % 2 + 1) * 64]
        for tile in range(8):
            at = slice(tile * 128, (tile + 1) * 128)
            block = (held[i, :, at] * mask_ref[0, i : i + 1, at]).T.astype(jnp.bfloat16)
            for half in range(2):
                stop = lax.rem(tile * 2 + half + 15 - y, 16) + 1
                out_ref[pl.ds(pl.multiple_of(i * 1088 + stop * 64, 64), 64), :] = block[half * 64 : (half + 1) * 64]


def finish(y, mask, mask0, outer, inner, pieces):
    return pl.pallas_call(
        finish_kernel,
        grid_spec=pltpu.PrefetchScalarGridSpec(
            num_scalar_prefetch=1,
            grid=(32 // STEP,),
            in_specs=[
                pl.BlockSpec((1, STEP, 1024), lambda i, y: (i, 0, 0)),
                pl.BlockSpec((STEP // 2, 1, 128), lambda i, y: (i, 0, 0)),
            ]
            + [
                pl.BlockSpec((4, STEP * NF, 256), lambda i, y: (0, i, 0)),
                pl.BlockSpec((4, 2 * NF, 256), lambda i, y: (0, 16 + i % 4, 0)),
                pl.BlockSpec((4, STEP * NF, 768), lambda i, y: (0, i, 0)),
            ]
            + [pl.BlockSpec((4, STEP * NF, 1024), lambda i, y: (0, i, 0)) for _ in pieces]
            + [pl.BlockSpec((4, 2 * NF, 1024), lambda i, y: (0, 16, 0)) for _ in pieces],
            out_specs=pl.BlockSpec((STEP * 1088, 128), lambda i, y: (i, 0)),
            scratch_shapes=[
                pltpu.VMEM((STEP, 128, 1024), jnp.float32),
                pltpu.VMEM((STEP // 2, 128, 128), jnp.float32),
            ],
        ),
        out_shape=jax.ShapeDtypeStruct((34816, 128), jnp.bfloat16),
        compiler_params=pltpu.CompilerParams(vmem_limit_bytes=60 * MB),
        cost_estimate=cost(9.0),
        name="finish",
    )(y, mask, mask0, outer, outer, inner, *pieces, *pieces)


def shift(block, axis, distance):
    size = lax.axis_size(axis)
    return lax.ppermute(block, axis, [(i, (i + distance) % size) for i in range(size)])


def tie(block, after):
    return block if after is None else lax.optimization_barrier((block, after))[0]


def hour_sum(value):
    total = value
    for zh, core in ((0, 1), (1, 0), (1, 1)):
        route = [(i, i ^ (zh * 2 + core)) for i in range(4)]
        total = total + lax.ppermute(value, ("zh", "core"), route)
    return total


def body(samples, gap_starts, valid_counts, owners, pair_mask):
    places = jnp.arange(L, dtype=jnp.int32)
    inside = places[None, :] < valid_counts[:, None]
    starts = gap_starts[:, :, None]
    holes = jnp.any((places[None, None, :] >= starts) & (places[None, None, :] < starts + GAPW), axis=1)
    valid = (inside & jnp.logical_not(holes)).astype(jnp.float32)
    member = (owners == jnp.arange(HGROUPS, dtype=jnp.int32)[None, :]).astype(jnp.float32)
    group_size = hour_sum(jnp.sum(member, axis=0))
    weight = jnp.sum(member / (HGROUPS * group_size)[None, :], axis=1)
    root = jnp.repeat(jnp.sqrt(weight), 32)[None, :]

    y = lax.axis_index("y").astype(jnp.int32)
    y_arg = y[None]
    mask = jnp.repeat(pair_mask.astype(jnp.float32), 2, axis=2)
    mask0 = mask[:, 0].reshape(16, 1, 128)
    mask = jnp.roll(mask[:, 1:], y + 1, axis=1).reshape(32 // STEP, STEP, 1024)

    spectra = whiten(normalize(samples.reshape(1024, L), valid), root)

    def transpose(block, after, name):
        with jax.named_scope(name):
            return lax.all_to_all(tie(block, after), ("zh", "core", "y"), 0, 0, tiled=True)

    def swap(part):
        with jax.named_scope(f"z{part}"):
            return shift(owns[part], "zl", 1)

    p0 = transpose(spectra[0], None, "p0")
    p1 = transpose(spectra[1], p0, "p1")
    x = lax.axis_index("x")

    def exchange(block, name):
        with jax.named_scope(name):
            return lax.all_to_all(block, "y", 0, 0, tiled=True)

    def choose(part):
        with jax.named_scope(f"x{part}"):
            return lax.optimization_barrier([jnp.where(x < d, swapped[part], owns[part]) for d in (1, 2, 3)])

    def gather(part, blocks, before, last):
        with jax.named_scope(f"x{part}"):
            return [shift(tie(block, last if d == 2 else before), "x", -d) for d, block in zip((1, 2, 3), blocks)]

    def do_cross(part, visitors, after):
        return cross(tie(owns[part], after), (*visitors, swapped[part]))

    owns = [assemble(p0, 0)]
    swapped = [swap(0)]
    chosen = choose(0)
    v0 = gather(0, chosen, None, None)
    a0 = outer(tie(owns[0], chosen), swapped[0])
    ya0 = exchange(tie(a0, p1), "yA0")
    owns.append(assemble(tie(p1, chosen), 0))
    swapped.append(swap(1))
    p23 = transpose(spectra[2], ya0, "p23")
    owns += [assemble(p23, 0), assemble(p23, 1)]
    swapped += [swap(2), swap(3)]
    c0 = inner(owns[0], v0)
    y0 = exchange(tie(c0, p23), "y0")
    v1 = gather(1, choose(1), None, c0)
    c1 = do_cross(1, v1, (c0, owns[2], owns[3]))
    y1 = exchange(tie(c1, y0), "y1")
    v2 = gather(2, choose(2), v0, c1)
    c2 = do_cross(2, v2, (c1, y0))
    y2 = exchange(tie(c2, y1), "y2")
    v3 = gather(3, choose(3), v1, c2)
    c3 = do_cross(3, v3, (c2, y1))
    y3 = exchange(tie(c3, y2), "y3")
    return finish(y_arg, mask, mask0, ya0, y0, (y1, y2, y3)).reshape(32, 17, 32, 2, 128)


def solution(mesh):
    fine = Mesh(mesh.devices.reshape(2, 4, 4, 2, 2), ("zl", "x", "y", "zh", "core"))
    chan, hour = ("zl", "x", "y"), ("zh", "core")
    placed = (
        P(hour, chan, None),
        P(hour, None),
        P(hour),
        P(hour, None),
        P(chan, None, None),
    )
    return jax.shard_map(
        body,
        mesh=fine,
        in_specs=placed,
        out_specs=P(chan, None, None, None, hour),
        check_vma=False,
    )
```

```python
import functools
import math

import jax
import jax.numpy as jnp
import ml_dtypes
import numpy as np
from jax import lax
from jax.experimental import pallas as pl
from jax.experimental.pallas import tpu as pltpu
from jax.sharding import Mesh, PartitionSpec as P

L = 1024
HGROUPS = 8
BINS = 512
GAPW = 32
RAMW = 64
SMW = 64
NF = 8
PARTS = 4
MB = 1024 * 1024


def band_np(length, half_width):
    places = np.arange(length)
    return (np.abs(places[:, None] - places[None, :]) <= half_width).astype(ml_dtypes.bfloat16)


def inverse_count_np(length, half_width):
    places = np.arange(length)
    upper = np.minimum(places + half_width, length - 1)
    lower = np.maximum(places - half_width, 0)
    return (1.0 / (upper - lower + 1)).astype(np.float32)


def dft_rows_np():
    phase = np.arange(BINS)[:, None] * np.arange(L)[None, :] % L
    angle = 2.0 * math.pi / L * phase
    return np.concatenate([np.cos(angle), -np.sin(angle)], axis=0).astype(ml_dtypes.bfloat16)


def taper_np():
    return (0.5 - 0.5 * np.cos(2.0 * math.pi / L * np.arange(L))).astype(np.float32)


def spread_np():
    table = np.zeros((256, 512), np.float32)
    c = np.arange(128)
    table[c, 2 * c] = 1
    table[128 + c, 2 * c + 1] = -1
    table[128 + c, 256 + 2 * c] = 1
    table[c, 256 + 2 * c + 1] = 1
    return table.astype(ml_dtypes.bfloat16)


def cost(us):
    return pl.CostEstimate(flops=int(us * 3.45e+10), bytes_accessed=int(us * 1.08e+08), transcendentals=0)


def dot(a, b, contract=((1,), (0,))):
    return lax.dot_general(a, b, (contract, ((), ())), preferred_element_type=jnp.float32)


def lanes(shape):
    return lax.broadcasted_iota(jnp.int32, shape, len(shape) - 1)


WROWS = 512


def level_kernel(x_ref, starts_ref, counts_ref, band_ref, taper_ref, icount_ref, out_ref):
    places = lanes((WROWS // 32, L))
    valid = places < counts_ref[...]
    for gap in range(starts_ref.shape[1]):
        start = starts_ref[:, gap : gap + 1]
        valid = valid & ((places < start) | (places >= start + GAPW))
    valid = valid.astype(jnp.float32)
    x = x_ref[...].astype(jnp.float32).reshape(WROWS // 32, 32, L) * valid[:, None, :]
    x = x.reshape(WROWS, L)
    level = dot(jnp.abs(x).astype(jnp.bfloat16), band_ref[...]) * icount_ref[...]
    out_ref[...] = (taper_ref[...] * x / (level + 1e-06)).astype(jnp.bfloat16)


def whole(*shape):
    return pl.BlockSpec(shape, lambda *i: (0,) * len(shape))


def normalize(rows, starts, counts):
    return pl.pallas_call(
        level_kernel,
        grid=(1024 // WROWS,),
        in_specs=[
            pl.BlockSpec((WROWS, L), lambda i: (i, 0)),
            pl.BlockSpec((WROWS // 32, starts.shape[1]), lambda i: (i, 0)),
            pl.BlockSpec((WROWS // 32, 1), lambda i: (i, 0)),
            whole(L, L),
            whole(1, L),
            whole(1, L),
        ],
        out_specs=pl.BlockSpec((WROWS, L), lambda i: (i, 0)),
        out_shape=jax.ShapeDtypeStruct((1024, L), jnp.bfloat16),
        compiler_params=pltpu.CompilerParams(vmem_limit_bytes=48 * MB),
        cost_estimate=cost(6.0),
        name="normalize",
    )(
        rows,
        starts,
        counts,
        jnp.asarray(band_np(L, RAMW)),
        jnp.asarray(taper_np()[None, :]),
        jnp.asarray(inverse_count_np(L, RAMW)[None, :]),
    )


def whiten_kernel(x_ref, root_ref, dft_ref, bband_ref, bcount_ref, out0, out1, out23, held):
    step = pl.program_id(0)
    spectrum = dot(dft_ref[...], x_ref[...], ((1,), (1,)))
    real, imag = spectrum[:BINS], spectrum[BINS:]
    power = real * real + imag * imag
    high = power.astype(jnp.bfloat16)
    low = (power - high.astype(jnp.float32)).astype(jnp.bfloat16)
    smooth = (dot(bband_ref[...], high) + dot(bband_ref[...], low)) * bcount_ref[...]
    factor = lax.rsqrt(smooth + 1e-06) * root_ref[...]
    real, imag = real * factor, imag * factor
    first = lanes((BINS, 128)) < 64
    for tile in range(WROWS // 128):
        re = real[:, tile * 128 : (tile + 1) * 128]
        im = imag[:, tile * 128 : (tile + 1) * 128]
        at = step * (WROWS // 64) + tile * 2
        held[pl.ds(at, 1)] = jnp.where(first, re, pltpu.roll(im, 64, 1))[None]
        held[pl.ds(at + 1, 1)] = jnp.where(first, pltpu.roll(re, 64, 1), im)[None]

    @pl.when(step == pl.num_programs(0) - 1)
    def _():
        for block in range(BINS // 64):
            part = held[:, block * 64 : (block + 1) * 64, :]
            part = jnp.swapaxes(part, 0, 1).astype(jnp.bfloat16).reshape(2, 32, 16, 128)
            out0[block * 2 : block * 2 + 2] = part[:, :NF]
            out1[block * 2 : block * 2 + 2] = part[:, NF : 2 * NF]
            out23[block * 2 : block * 2 + 2] = part[:, 2 * NF :]


def whiten(rows, root):
    return pl.pallas_call(
        whiten_kernel,
        grid=(1024 // WROWS,),
        in_specs=[
            pl.BlockSpec((WROWS, L), lambda i: (i, 0)),
            pl.BlockSpec((1, WROWS), lambda i: (0, i)),
            whole(2 * BINS, L),
            whole(BINS, BINS),
            whole(BINS, 1),
        ],
        out_specs=[whole(16, NF, 16, 128), whole(16, NF, 16, 128), whole(16, 2 * NF, 16, 128)],
        out_shape=[
            jax.ShapeDtypeStruct((16, NF, 16, 128), jnp.bfloat16),
            jax.ShapeDtypeStruct((16, NF, 16, 128), jnp.bfloat16),
            jax.ShapeDtypeStruct((16, 2 * NF, 16, 128), jnp.bfloat16),
        ],
        scratch_shapes=[pltpu.VMEM((16, BINS, 128), jnp.float32)],
        compiler_params=pltpu.CompilerParams(vmem_limit_bytes=48 * MB),
        cost_estimate=cost(9.0),
        name="whiten",
    )(
        rows,
        root,
        jnp.asarray(dft_rows_np()),
        jnp.asarray(band_np(BINS, SMW)),
        jnp.asarray(inverse_count_np(BINS, SMW)[:, None]),
    )


def assemble_kernel(piece_ref, *out_refs):
    for part, out_ref in enumerate(out_refs):
        assemble_part(piece_ref.at[:, part * NF : (part + 1) * NF], out_ref)


def assemble_part(piece_ref, out_ref):
    count = NF
    pieces = []
    for y in range(4):
        both = [piece_ref[h * 4 + y].astype(jnp.float32) for h in range(4)]
        pieces.append(jnp.stack(both, axis=1).reshape(count * 64, 128))
    group = lanes((count * 64, 128)) // 32
    for part in range(2):
        for bit in range(2):
            block = part * 2 + bit
            total = None
            for y in range(4):
                shift = (32 * (y - block)) % 128
                moved = pieces[y] if shift == 0 else pltpu.roll(pieces[y], shift, 1)
                total = moved if total is None else jnp.where(group == y, moved, total)
            out_ref[:, bit * 64 : (bit + 1) * 64, part * 128 : (part + 1) * 128] = total.reshape(
                count, 64, 128
            ).astype(jnp.bfloat16)


def assemble(pieces):
    parts = pieces.shape[1] // NF
    return pl.pallas_call(
        assemble_kernel,
        grid=(1,),
        in_specs=[whole(*pieces.shape)],
        out_specs=[whole(NF, 128, 256)] * parts,
        out_shape=[jax.ShapeDtypeStruct((NF, 128, 256), jnp.bfloat16)] * parts,
        compiler_params=pltpu.CompilerParams(vmem_limit_bytes=32 * MB),
        cost_estimate=cost(0.8 * parts),
        name="assemble",
    )(pieces)


def own_side(own):
    return jnp.concatenate([own[:, :128].T, own[:, 128:].T], axis=1)


def visiting_side(block, spread):
    wide = dot(block, spread).astype(jnp.bfloat16)
    return jnp.concatenate([wide[:, :256], wide[:, 256:]], axis=0)


def cross_kernel(own_ref, v1_ref, v2_ref, v3_ref, v4_ref, spread_ref, out, held, zero_stop, wide):
    group = lanes((32, 256)) // 64
    first = lanes((32, 128)) < 64
    for d, visitor in enumerate((own_ref, v1_ref, v2_ref, v3_ref, v4_ref)):
        wide[d] = dot(visitor[...].reshape(NF * 128, 256), spread_ref[...]).astype(jnp.bfloat16)

    def right(d, f):
        rows = wide[d, f * 128 : (f + 1) * 128]
        return jnp.concatenate([rows[:, :256], rows[:, 256:]], axis=0)

    for f in range(NF):
        left = own_side(own_ref[f])
        near = dot(left, right(0, f))
        far = dot(left, right(4, f))
        for m in range(1, 4):
            held[f, :, m * 256 : (m + 1) * 256] = dot(left, right(m, f))
        for g in range(4):
            at = slice(g * 32, (g + 1) * 32)
            held[f, at, :256] = jnp.where(group <= g, far[at], near[at])
            tile = near[at, (g // 2) * 128 : (g // 2 + 1) * 128]
            turned = pltpu.roll(tile, 64, 1)
            zero_stop[f, at, :] = jnp.where(first, tile, turned) if g % 2 == 0 else jnp.where(first, turned, tile)
    pair = lanes((16, NF, 128)) < 64
    for g in range(4):
        for i in range(0, 32, 8):
            rows = jnp.swapaxes(held[:, g * 32 + i : g * 32 + i + 8, :], 0, 1)
            out[g, i * NF : (i + 8) * NF, :] = rows.reshape(8 * NF, 1024).astype(jnp.bfloat16)
        rows = jnp.swapaxes(zero_stop[:, g * 32 : (g + 1) * 32, :], 0, 1).reshape(16, 2, NF, 128)
        rows = jnp.where(pair, rows[:, 0], rows[:, 1])
        for u in range(8):
            both = jnp.concatenate([rows[2 * u], rows[2 * u + 1]], axis=0)
            out[g, 32 * NF :, u * 128 : (u + 1) * 128] = both.astype(jnp.bfloat16)


def cross(own, visitors):
    return pl.pallas_call(
        cross_kernel,
        grid=(1,),
        in_specs=[whole(NF, 128, 256) for _ in range(5)] + [whole(256, 512)],
        out_specs=whole(4, 34 * NF, 1024),
        scratch_shapes=[
            pltpu.VMEM((NF, 128, 1024), jnp.float32),
            pltpu.VMEM((NF, 128, 128), jnp.float32),
            pltpu.VMEM((5, NF * 128, 512), jnp.bfloat16),
        ],
        out_shape=jax.ShapeDtypeStruct((4, 34 * NF, 1024), jnp.bfloat16),
        compiler_params=pltpu.CompilerParams(vmem_limit_bytes=60 * MB),
        cost_estimate=cost(10.0),
        name="cross",
    )(own, *visitors, jnp.asarray(spread_np()))


def outer_kernel(own_ref, v4_ref, spread_ref, out, held, zero_stop, wide):
    group = lanes((32, 256)) // 64
    first = lanes((32, 128)) < 64
    for d, visitor in enumerate((own_ref, v4_ref)):
        wide[d] = dot(visitor[...].reshape(NF * 128, 256), spread_ref[...]).astype(jnp.bfloat16)

    def right(d, f):
        rows = wide[d, f * 128 : (f + 1) * 128]
        return jnp.concatenate([rows[:, :256], rows[:, 256:]], axis=0)

    for f in range(NF):
        left = own_side(own_ref[f])
        near = dot(left, right(0, f))
        far = dot(left, right(1, f))
        for g in range(4):
            at = slice(g * 32, (g + 1) * 32)
            held[f, at, :] = jnp.where(group <= g, far[at], near[at])
            tile = near[at, (g // 2) * 128 : (g // 2 + 1) * 128]
            turned = pltpu.roll(tile, 64, 1)
            zero_stop[f, at, :] = jnp.where(first, tile, turned) if g % 2 == 0 else jnp.where(first, turned, tile)
    pair = lanes((16, NF, 128)) < 64
    for g in range(4):
        for i in range(0, 32, 8):
            rows = jnp.swapaxes(held[:, g * 32 + i : g * 32 + i + 8, :], 0, 1)
            out[g, i * NF : (i + 8) * NF, :] = rows.reshape(8 * NF, 256).astype(jnp.bfloat16)
        rows = jnp.swapaxes(zero_stop[:, g * 32 : (g + 1) * 32, :], 0, 1).reshape(16, 2, NF, 128)
        rows = jnp.where(pair, rows[:, 0], rows[:, 1]).reshape(16 * NF, 128)
        out[g, 32 * NF :, :128] = rows[: 8 * NF].astype(jnp.bfloat16)
        out[g, 32 * NF :, 128:] = rows[8 * NF :].astype(jnp.bfloat16)


def inner_kernel(own_ref, v1_ref, v2_ref, v3_ref, spread_ref, out, held, wide):
    for d, visitor in enumerate((v1_ref, v2_ref, v3_ref)):
        wide[d] = dot(visitor[...].reshape(NF * 128, 256), spread_ref[...]).astype(jnp.bfloat16)
    for f in range(NF):
        left = own_side(own_ref[f])
        for m in range(3):
            rows = wide[m, f * 128 : (f + 1) * 128]
            right = jnp.concatenate([rows[:, :256], rows[:, 256:]], axis=0)
            held[f, :, m * 256 : (m + 1) * 256] = dot(left, right)
    for g in range(4):
        for i in range(0, 32, 8):
            rows = jnp.swapaxes(held[:, g * 32 + i : g * 32 + i + 8, :], 0, 1)
            out[g, i * NF : (i + 8) * NF, :] = rows.reshape(8 * NF, 768).astype(jnp.bfloat16)


def early(kernel, name, us, shape, scratch, *blocks):
    return pl.pallas_call(
        kernel,
        grid=(1,),
        in_specs=[whole(NF, 128, 256) for _ in blocks] + [whole(256, 512)],
        out_specs=whole(*shape),
        scratch_shapes=scratch,
        out_shape=jax.ShapeDtypeStruct(shape, jnp.bfloat16),
        compiler_params=pltpu.CompilerParams(vmem_limit_bytes=60 * MB),
        cost_estimate=cost(us),
        name=name,
    )(*blocks, jnp.asarray(spread_np()))


def outer(own, opposite):
    scratch = [
        pltpu.VMEM((NF, 128, 256), jnp.float32),
        pltpu.VMEM((NF, 128, 128), jnp.float32),
        pltpu.VMEM((2, NF * 128, 512), jnp.bfloat16),
    ]
    return early(outer_kernel, "outer", 3.0, (4, 40 * NF, 256), scratch, own, opposite)


def inner(own, visitors):
    scratch = [
        pltpu.VMEM((NF, 128, 768), jnp.float32),
        pltpu.VMEM((3, NF * 128, 512), jnp.bfloat16),
    ]
    return early(inner_kernel, "inner", 5.0, (4, 32 * NF, 768), scratch, own, *visitors)


STEP = 4


def finish_kernel(y_ref, mask_ref, mask0_ref, outer_ref, outer0_ref, inner_ref, *rest):
    pieces, zeros, last, last0, (out_ref, held, held0) = rest[:2], rest[2:4], rest[4:8], rest[8:12], rest[12:]
    step = pl.program_id(0)
    y = y_ref[0]
    lane_at = pl.multiple_of(step * 128, 128)
    first_at = pl.multiple_of(step // 4 * 128, 128)
    for source in range(4):
        row = slice(source * 32, source * 32 + NF)
        both = outer_ref[source].astype(jnp.float32)
        others = inner_ref[source].astype(jnp.float32)
        for i in range(STEP):
            held[i, row, :256] = both[i * NF : (i + 1) * NF]
            held[i, row, 256:] = others[i * NF : (i + 1) * NF]
        both = outer0_ref[source, :, pl.ds(first_at, 128)].astype(jnp.float32)
        for pair in range(2):
            held0[pair, row, :] = both[pair * NF : (pair + 1) * NF]
        for part in range(1, PARTS - 1):
            row = slice(source * 32 + part * NF, source * 32 + (part + 1) * NF)
            both = pieces[part - 1][source].astype(jnp.float32)
            for i in range(STEP):
                held[i, row, :] = both[i * NF : (i + 1) * NF]
            both = zeros[part - 1][source, :, pl.ds(lane_at, 128)].astype(jnp.float32)
            for pair in range(2):
                held0[pair, row, :] = both[pair * NF : (pair + 1) * NF]
    for s in range(4):
        row = pl.ds(pl.multiple_of(lax.rem(y + 4 - s, 4) * 32 + (PARTS - 1) * NF, NF), NF)
        both = last[s][...].astype(jnp.float32)
        for i in range(STEP):
            held[i, row, :] = both[i * NF : (i + 1) * NF]
        both = last0[s][:, pl.ds(lane_at, 128)].astype(jnp.float32)
        for pair in range(2):
            held0[pair, row, :] = both[pair * NF : (pair + 1) * NF]
    for i in range(STEP):
        if i % 2 == 0:
            zero = (held0[i // 2] * mask0_ref[i // 2]).T.astype(jnp.bfloat16)
        out_ref[i * 1088 : i * 1088 + 64, :] = zero[i % 2 * 64 : (i % 2 + 1) * 64]
        for tile in range(8):
            at = slice(tile * 128, (tile + 1) * 128)
            block = (held[i, :, at] * mask_ref[0, i : i + 1, at]).T.astype(jnp.bfloat16)
            for half in range(2):
                stop = lax.rem(tile * 2 + half + 15 - y, 16) + 1
                out_ref[pl.ds(pl.multiple_of(i * 1088 + stop * 64, 64), 64), :] = block[half * 64 : (half + 1) * 64]


def finish(y, mask, mask0, outer, inner, pieces, last):
    return pl.pallas_call(
        finish_kernel,
        grid_spec=pltpu.PrefetchScalarGridSpec(
            num_scalar_prefetch=1,
            grid=(32 // STEP,),
            in_specs=[
                pl.BlockSpec((1, STEP, 1024), lambda i, y: (i, 0, 0)),
                pl.BlockSpec((STEP // 2, 1, 128), lambda i, y: (i, 0, 0)),
            ]
            + [
                pl.BlockSpec((4, STEP * NF, 256), lambda i, y: (0, i, 0)),
                pl.BlockSpec((4, 2 * NF, 256), lambda i, y: (0, 16 + i % 4, 0)),
                pl.BlockSpec((4, STEP * NF, 768), lambda i, y: (0, i, 0)),
            ]
            + [pl.BlockSpec((4, STEP * NF, 1024), lambda i, y: (0, i, 0)) for _ in pieces]
            + [pl.BlockSpec((4, 2 * NF, 1024), lambda i, y: (0, 16, 0)) for _ in pieces]
            + [pl.BlockSpec((STEP * NF, 1024), lambda i, y: (i, 0)) for _ in last]
            + [pl.BlockSpec((2 * NF, 1024), lambda i, y: (16, 0)) for _ in last],
            out_specs=pl.BlockSpec((STEP * 1088, 128), lambda i, y: (i, 0)),
            scratch_shapes=[
                pltpu.VMEM((STEP, 128, 1024), jnp.float32),
                pltpu.VMEM((STEP // 2, 128, 128), jnp.float32),
            ],
        ),
        out_shape=jax.ShapeDtypeStruct((34816, 128), jnp.bfloat16),
        compiler_params=pltpu.CompilerParams(vmem_limit_bytes=60 * MB),
        cost_estimate=cost(9.0),
        name="finish",
    )(y, mask, mask0, outer, outer, inner, *pieces, *pieces, *last, *last)


def shift(block, axis, distance):
    size = lax.axis_size(axis)
    return lax.ppermute(block, axis, [(i, (i + distance) % size) for i in range(size)])


def tie(block, after):
    return block if after is None else lax.optimization_barrier((block, after))[0]


def hour_sum(value):
    total = value
    for zh, core in ((0, 1), (1, 0), (1, 1)):
        route = [(i, i ^ (zh * 2 + core)) for i in range(4)]
        total = total + lax.ppermute(value, ("zh", "core"), route)
    return total


def body(samples, gap_starts, valid_counts, owners, pair_mask):
    member = (owners == jnp.arange(HGROUPS, dtype=jnp.int32)[None, :]).astype(jnp.float32)
    group_size = hour_sum(jnp.sum(member, axis=0))
    weight = jnp.sum(member / (HGROUPS * group_size)[None, :], axis=1)
    root = jnp.repeat(jnp.sqrt(weight), 32)[None, :]

    y = lax.axis_index("y").astype(jnp.int32)
    y_arg = y[None]
    mask = jnp.repeat(pair_mask.astype(jnp.float32), 2, axis=2)
    mask0 = mask[:, 0].reshape(16, 1, 128)
    mask = jnp.roll(mask[:, 1:], y + 1, axis=1).reshape(32 // STEP, STEP, 1024)

    spectra = whiten(normalize(samples.reshape(1024, L), gap_starts, valid_counts[:, None]), root)

    def transpose(block, after, name):
        with jax.named_scope(name):
            return lax.all_to_all(tie(block, after), ("zh", "core", "y"), 0, 0, tiled=True)

    def swap(part):
        with jax.named_scope(f"z{part}"):
            return shift(owns[part], "zl", 1)

    p0 = transpose(spectra[0], None, "p0")
    p1 = transpose(spectra[1], p0, "p1")
    x = lax.axis_index("x")

    def exchange(block, name):
        with jax.named_scope(name):
            return lax.all_to_all(block, "y", 0, 0, tiled=True)

    def choose(part):
        with jax.named_scope(f"x{part}"):
            return lax.optimization_barrier([jnp.where(x < d, swapped[part], owns[part]) for d in (1, 2, 3)])

    def gather(part, blocks, before, last):
        with jax.named_scope(f"x{part}"):
            return [shift(tie(block, last if d == 2 else before), "x", -d) for d, block in zip((1, 2, 3), blocks)]

    def do_cross(part, visitors, after):
        return cross(tie(owns[part], after), (*visitors, swapped[part]))

    owns = assemble(p0)
    swapped = [swap(0)]
    chosen = choose(0)
    v0 = gather(0, chosen, None, None)
    a0 = outer(tie(owns[0], chosen), swapped[0])
    ya0 = exchange(tie(a0, p1), "yA0")
    owns += assemble(tie(p1, chosen))
    swapped.append(swap(1))
    p23 = transpose(spectra[2], ya0, "p23")
    owns += assemble(p23)
    swapped += [swap(2), swap(3)]
    c0 = inner(owns[0], v0)
    y0 = exchange(tie(c0, p23), "y0")
    v1 = gather(1, choose(1), None, c0)
    c1 = do_cross(1, v1, (c0, owns[2], owns[3]))
    y1 = exchange(tie(c1, y0), "y1")
    v2 = gather(2, choose(2), v0, c1)
    c2 = do_cross(2, v2, (c1, y0))
    y2 = exchange(tie(c2, y1), "y2")
    v3 = gather(3, choose(3), v1, c2)
    c3 = do_cross(3, v3, (c2, y1))
    y3 = [lax.dynamic_index_in_dim(c3, (y + s) % 4, 0, keepdims=False) for s in range(4)]
    with jax.named_scope("y3"):
        y3 = [y3[0]] + [shift(y3[s], "y", s) for s in range(1, 4)]
    return finish(y_arg, mask, mask0, ya0, y0, (y1, y2), y3).reshape(32, 17, 32, 2, 128)


def solution(mesh):
    fine = Mesh(mesh.devices.reshape(2, 4, 4, 2, 2), ("zl", "x", "y", "zh", "core"))
    chan, hour = ("zl", "x", "y"), ("zh", "core")
    placed = (
        P(hour, chan, None),
        P(hour, None),
        P(hour),
        P(hour, None),
        P(chan, None, None),
    )
    return jax.shard_map(
        body,
        mesh=fine,
        in_specs=placed,
        out_specs=P(chan, None, None, None, hour),
        check_vma=False,
    )
```

```python
import functools
import math

import jax
import jax.numpy as jnp
import ml_dtypes
import numpy as np
from jax import lax
from jax.experimental import pallas as pl
from jax.experimental.pallas import tpu as pltpu
from jax.sharding import Mesh, PartitionSpec as P

L = 1024
HGROUPS = 8
BINS = 512
GAPW = 32
RAMW = 64
SMW = 64
NF = 8
PARTS = 4
MB = 1024 * 1024


def band_np(length, half_width):
    places = np.arange(length)
    return (np.abs(places[:, None] - places[None, :]) <= half_width).astype(ml_dtypes.bfloat16)


def inverse_count_np(length, half_width):
    places = np.arange(length)
    upper = np.minimum(places + half_width, length - 1)
    lower = np.maximum(places - half_width, 0)
    return (1.0 / (upper - lower + 1)).astype(np.float32)


def dft_rows_np():
    phase = np.arange(BINS)[:, None] * np.arange(L)[None, :] % L
    angle = 2.0 * math.pi / L * phase
    return np.concatenate([np.cos(angle), -np.sin(angle)], axis=0).astype(ml_dtypes.bfloat16)


def taper_np():
    return (0.5 - 0.5 * np.cos(2.0 * math.pi / L * np.arange(L))).astype(np.float32)


def spread_np():
    table = np.zeros((256, 512), np.float32)
    c = np.arange(128)
    table[c, 2 * c] = 1
    table[128 + c, 2 * c + 1] = -1
    table[128 + c, 256 + 2 * c] = 1
    table[c, 256 + 2 * c + 1] = 1
    return table.astype(ml_dtypes.bfloat16)


def cost(us):
    return pl.CostEstimate(flops=int(us * 3.45e+10), bytes_accessed=int(us * 1.08e+08), transcendentals=0)


def dot(a, b, contract=((1,), (0,))):
    return lax.dot_general(a, b, (contract, ((), ())), preferred_element_type=jnp.float32)


def lanes(shape):
    return lax.broadcasted_iota(jnp.int32, shape, len(shape) - 1)


WROWS = 512


def level_kernel(x_ref, starts_ref, counts_ref, band_ref, taper_ref, icount_ref, out_ref):
    places = lanes((WROWS // 32, L))
    valid = places < counts_ref[...]
    for gap in range(starts_ref.shape[1]):
        start = starts_ref[:, gap : gap + 1]
        valid = valid & ((places < start) | (places >= start + GAPW))
    valid = valid.astype(jnp.float32)
    x = x_ref[...].astype(jnp.float32).reshape(WROWS // 32, 32, L) * valid[:, None, :]
    x = x.reshape(WROWS, L)
    level = dot(jnp.abs(x).astype(jnp.bfloat16), band_ref[...]) * icount_ref[...]
    out_ref[...] = (taper_ref[...] * x / (level + 1e-06)).astype(jnp.bfloat16)


def whole(*shape):
    return pl.BlockSpec(shape, lambda *i: (0,) * len(shape))


def normalize(rows, starts, counts):
    return pl.pallas_call(
        level_kernel,
        grid=(1024 // WROWS,),
        in_specs=[
            pl.BlockSpec((WROWS, L), lambda i: (i, 0)),
            pl.BlockSpec((WROWS // 32, starts.shape[1]), lambda i: (i, 0)),
            pl.BlockSpec((WROWS // 32, 1), lambda i: (i, 0)),
            whole(L, L),
            whole(1, L),
            whole(1, L),
        ],
        out_specs=pl.BlockSpec((WROWS, L), lambda i: (i, 0)),
        out_shape=jax.ShapeDtypeStruct((1024, L), jnp.bfloat16),
        compiler_params=pltpu.CompilerParams(vmem_limit_bytes=48 * MB),
        cost_estimate=cost(6.0),
        name="normalize",
    )(
        rows,
        starts,
        counts,
        jnp.asarray(band_np(L, RAMW)),
        jnp.asarray(taper_np()[None, :]),
        jnp.asarray(inverse_count_np(L, RAMW)[None, :]),
    )


def whiten_kernel(x_ref, root_ref, dft_ref, bband_ref, bcount_ref, out0, out1, out23, held):
    step = pl.program_id(0)
    spectrum = dot(dft_ref[...], x_ref[...], ((1,), (1,)))
    real, imag = spectrum[:BINS], spectrum[BINS:]
    power = real * real + imag * imag
    high = power.astype(jnp.bfloat16)
    low = (power - high.astype(jnp.float32)).astype(jnp.bfloat16)
    smooth = (dot(bband_ref[...], high) + dot(bband_ref[...], low)) * bcount_ref[...]
    factor = lax.rsqrt(smooth + 1e-06) * root_ref[...]
    real, imag = real * factor, imag * factor
    first = lanes((BINS, 128)) < 64
    for tile in range(WROWS // 128):
        re = real[:, tile * 128 : (tile + 1) * 128]
        im = imag[:, tile * 128 : (tile + 1) * 128]
        at = step * (WROWS // 64) + tile * 2
        held[pl.ds(at, 1)] = jnp.where(first, re, pltpu.roll(im, 64, 1))[None]
        held[pl.ds(at + 1, 1)] = jnp.where(first, pltpu.roll(re, 64, 1), im)[None]

    @pl.when(step == pl.num_programs(0) - 1)
    def _():
        for block in range(BINS // 64):
            part = held[:, block * 64 : (block + 1) * 64, :]
            part = jnp.swapaxes(part, 0, 1).astype(jnp.bfloat16).reshape(2, 32, 16, 128)
            out0[block * 2 : block * 2 + 2] = part[:, :NF]
            out1[block * 2 : block * 2 + 2] = part[:, NF : 2 * NF]
            out23[block * 2 : block * 2 + 2] = part[:, 2 * NF :]


def whiten(rows, root):
    return pl.pallas_call(
        whiten_kernel,
        grid=(1024 // WROWS,),
        in_specs=[
            pl.BlockSpec((WROWS, L), lambda i: (i, 0)),
            pl.BlockSpec((1, WROWS), lambda i: (0, i)),
            whole(2 * BINS, L),
            whole(BINS, BINS),
            whole(BINS, 1),
        ],
        out_specs=[whole(16, NF, 16, 128), whole(16, NF, 16, 128), whole(16, 2 * NF, 16, 128)],
        out_shape=[
            jax.ShapeDtypeStruct((16, NF, 16, 128), jnp.bfloat16),
            jax.ShapeDtypeStruct((16, NF, 16, 128), jnp.bfloat16),
            jax.ShapeDtypeStruct((16, 2 * NF, 16, 128), jnp.bfloat16),
        ],
        scratch_shapes=[pltpu.VMEM((16, BINS, 128), jnp.float32)],
        compiler_params=pltpu.CompilerParams(vmem_limit_bytes=48 * MB),
        cost_estimate=cost(9.0),
        name="whiten",
    )(
        rows,
        root,
        jnp.asarray(dft_rows_np()),
        jnp.asarray(band_np(BINS, SMW)),
        jnp.asarray(inverse_count_np(BINS, SMW)[:, None]),
    )


def assemble_kernel(piece_ref, *out_refs):
    for part, out_ref in enumerate(out_refs):
        assemble_part(piece_ref.at[:, part * NF : (part + 1) * NF], out_ref)


def assemble_part(piece_ref, out_ref):
    count = NF
    pieces = []
    for y in range(4):
        both = [piece_ref[h * 4 + y].astype(jnp.float32) for h in range(4)]
        pieces.append(jnp.stack(both, axis=1).reshape(count * 64, 128))
    group = lanes((count * 64, 128)) // 32
    for part in range(2):
        for bit in range(2):
            block = part * 2 + bit
            total = None
            for y in range(4):
                shift = (32 * (y - block)) % 128
                moved = pieces[y] if shift == 0 else pltpu.roll(pieces[y], shift, 1)
                total = moved if total is None else jnp.where(group == y, moved, total)
            out_ref[:, bit * 64 : (bit + 1) * 64, part * 128 : (part + 1) * 128] = total.reshape(
                count, 64, 128
            ).astype(jnp.bfloat16)


def assemble(pieces):
    parts = pieces.shape[1] // NF
    return pl.pallas_call(
        assemble_kernel,
        grid=(1,),
        in_specs=[whole(*pieces.shape)],
        out_specs=[whole(NF, 128, 256)] * parts,
        out_shape=[jax.ShapeDtypeStruct((NF, 128, 256), jnp.bfloat16)] * parts,
        compiler_params=pltpu.CompilerParams(vmem_limit_bytes=32 * MB),
        cost_estimate=cost(0.8 * parts),
        name="assemble",
    )(pieces)


def own_side(own):
    return jnp.concatenate([own[:, :128].T, own[:, 128:].T], axis=1)


def visiting_side(block, spread):
    wide = dot(block, spread).astype(jnp.bfloat16)
    return jnp.concatenate([wide[:, :256], wide[:, 256:]], axis=0)


def cross_kernel(own_ref, v1_ref, v2_ref, v3_ref, v4_ref, spread_ref, out, held, zero_stop, wide):
    group = lanes((32, 256)) // 64
    first = lanes((32, 128)) < 64
    for d, visitor in enumerate((own_ref, v1_ref, v2_ref, v3_ref, v4_ref)):
        wide[d] = dot(visitor[...].reshape(NF * 128, 256), spread_ref[...]).astype(jnp.bfloat16)

    def right(d, f):
        rows = wide[d, f * 128 : (f + 1) * 128]
        return jnp.concatenate([rows[:, :256], rows[:, 256:]], axis=0)

    for f in range(NF):
        left = own_side(own_ref[f])
        near = dot(left, right(0, f))
        far = dot(left, right(4, f))
        for m in range(1, 4):
            held[f, :, m * 256 : (m + 1) * 256] = dot(left, right(m, f))
        for g in range(4):
            at = slice(g * 32, (g + 1) * 32)
            held[f, at, :256] = jnp.where(group <= g, far[at], near[at])
            tile = near[at, (g // 2) * 128 : (g // 2 + 1) * 128]
            turned = pltpu.roll(tile, 64, 1)
            zero_stop[f, at, :] = jnp.where(first, tile, turned) if g % 2 == 0 else jnp.where(first, turned, tile)
    pair = lanes((16, NF, 128)) < 64
    for g in range(4):
        for i in range(0, 32, 8):
            rows = jnp.swapaxes(held[:, g * 32 + i : g * 32 + i + 8, :], 0, 1)
            out[g, i * NF : (i + 8) * NF, :] = rows.reshape(8 * NF, 1024).astype(jnp.bfloat16)
        rows = jnp.swapaxes(zero_stop[:, g * 32 : (g + 1) * 32, :], 0, 1).reshape(16, 2, NF, 128)
        rows = jnp.where(pair, rows[:, 0], rows[:, 1])
        for u in range(8):
            both = jnp.concatenate([rows[2 * u], rows[2 * u + 1]], axis=0)
            out[g, 32 * NF :, u * 128 : (u + 1) * 128] = both.astype(jnp.bfloat16)


def cross(own, visitors):
    return pl.pallas_call(
        cross_kernel,
        grid=(1,),
        in_specs=[whole(NF, 128, 256) for _ in range(5)] + [whole(256, 512)],
        out_specs=whole(4, 34 * NF, 1024),
        scratch_shapes=[
            pltpu.VMEM((NF, 128, 1024), jnp.float32),
            pltpu.VMEM((NF, 128, 128), jnp.float32),
            pltpu.VMEM((5, NF * 128, 512), jnp.bfloat16),
        ],
        out_shape=jax.ShapeDtypeStruct((4, 34 * NF, 1024), jnp.bfloat16),
        compiler_params=pltpu.CompilerParams(vmem_limit_bytes=60 * MB),
        cost_estimate=cost(10.0),
        name="cross",
    )(own, *visitors, jnp.asarray(spread_np()))


def outer_kernel(own_ref, v4_ref, spread_ref, out, held, zero_stop, wide):
    group = lanes((32, 256)) // 64
    first = lanes((32, 128)) < 64
    for d, visitor in enumerate((own_ref, v4_ref)):
        wide[d] = dot(visitor[...].reshape(NF * 128, 256), spread_ref[...]).astype(jnp.bfloat16)

    def right(d, f):
        rows = wide[d, f * 128 : (f + 1) * 128]
        return jnp.concatenate([rows[:, :256], rows[:, 256:]], axis=0)

    for f in range(NF):
        left = own_side(own_ref[f])
        near = dot(left, right(0, f))
        far = dot(left, right(1, f))
        for g in range(4):
            at = slice(g * 32, (g + 1) * 32)
            held[f, at, :] = jnp.where(group <= g, far[at], near[at])
            tile = near[at, (g // 2) * 128 : (g // 2 + 1) * 128]
            turned = pltpu.roll(tile, 64, 1)
            zero_stop[f, at, :] = jnp.where(first, tile, turned) if g % 2 == 0 else jnp.where(first, turned, tile)
    pair = lanes((16, NF, 128)) < 64
    for g in range(4):
        for i in range(0, 32, 8):
            rows = jnp.swapaxes(held[:, g * 32 + i : g * 32 + i + 8, :], 0, 1)
            out[g, i * NF : (i + 8) * NF, :] = rows.reshape(8 * NF, 256).astype(jnp.bfloat16)
        rows = jnp.swapaxes(zero_stop[:, g * 32 : (g + 1) * 32, :], 0, 1).reshape(16, 2, NF, 128)
        rows = jnp.where(pair, rows[:, 0], rows[:, 1]).reshape(16 * NF, 128)
        out[g, 32 * NF :, :128] = rows[: 8 * NF].astype(jnp.bfloat16)
        out[g, 32 * NF :, 128:] = rows[8 * NF :].astype(jnp.bfloat16)


def inner_kernel(own_ref, v1_ref, v2_ref, v3_ref, spread_ref, out, held, wide):
    for d, visitor in enumerate((v1_ref, v2_ref, v3_ref)):
        wide[d] = dot(visitor[...].reshape(NF * 128, 256), spread_ref[...]).astype(jnp.bfloat16)
    for f in range(NF):
        left = own_side(own_ref[f])
        for m in range(3):
            rows = wide[m, f * 128 : (f + 1) * 128]
            right = jnp.concatenate([rows[:, :256], rows[:, 256:]], axis=0)
            held[f, :, m * 256 : (m + 1) * 256] = dot(left, right)
    for g in range(4):
        for i in range(0, 32, 8):
            rows = jnp.swapaxes(held[:, g * 32 + i : g * 32 + i + 8, :], 0, 1)
            out[g, i * NF : (i + 8) * NF, :] = rows.reshape(8 * NF, 768).astype(jnp.bfloat16)


def early(kernel, name, us, shape, scratch, *blocks):
    return pl.pallas_call(
        kernel,
        grid=(1,),
        in_specs=[whole(NF, 128, 256) for _ in blocks] + [whole(256, 512)],
        out_specs=whole(*shape),
        scratch_shapes=scratch,
        out_shape=jax.ShapeDtypeStruct(shape, jnp.bfloat16),
        compiler_params=pltpu.CompilerParams(vmem_limit_bytes=60 * MB),
        cost_estimate=cost(us),
        name=name,
    )(*blocks, jnp.asarray(spread_np()))


def outer(own, opposite):
    scratch = [
        pltpu.VMEM((NF, 128, 256), jnp.float32),
        pltpu.VMEM((NF, 128, 128), jnp.float32),
        pltpu.VMEM((2, NF * 128, 512), jnp.bfloat16),
    ]
    return early(outer_kernel, "outer", 3.0, (4, 40 * NF, 256), scratch, own, opposite)


def inner(own, visitors):
    scratch = [
        pltpu.VMEM((NF, 128, 768), jnp.float32),
        pltpu.VMEM((3, NF * 128, 512), jnp.bfloat16),
    ]
    return early(inner_kernel, "inner", 5.0, (4, 32 * NF, 768), scratch, own, *visitors)


STEP = 4


def finish_kernel(y_ref, mask_ref, mask0_ref, outer_ref, outer0_ref, inner_ref, *rest):
    pieces, zeros, last, last0, (out_ref, held, held0) = rest[:1], rest[1:2], rest[2:10], rest[10:18], rest[18:]
    step = pl.program_id(0)
    y = y_ref[0]
    lane_at = pl.multiple_of(step * 128, 128)
    first_at = pl.multiple_of(step // 4 * 128, 128)
    for source in range(4):
        row = slice(source * 32, source * 32 + NF)
        both = outer_ref[source].astype(jnp.float32)
        others = inner_ref[source].astype(jnp.float32)
        for i in range(STEP):
            held[i, row, :256] = both[i * NF : (i + 1) * NF]
            held[i, row, 256:] = others[i * NF : (i + 1) * NF]
        both = outer0_ref[source, :, pl.ds(first_at, 128)].astype(jnp.float32)
        for pair in range(2):
            held0[pair, row, :] = both[pair * NF : (pair + 1) * NF]
        for part in range(1, PARTS - 2):
            row = slice(source * 32 + part * NF, source * 32 + (part + 1) * NF)
            both = pieces[part - 1][source].astype(jnp.float32)
            for i in range(STEP):
                held[i, row, :] = both[i * NF : (i + 1) * NF]
            both = zeros[part - 1][source, :, pl.ds(lane_at, 128)].astype(jnp.float32)
            for pair in range(2):
                held0[pair, row, :] = both[pair * NF : (pair + 1) * NF]
    for s in range(8):
        part = PARTS - 2 + s // 4
        row = pl.ds(pl.multiple_of(lax.rem(y + 4 - s % 4, 4) * 32 + part * NF, NF), NF)
        both = last[s][...].astype(jnp.float32)
        for i in range(STEP):
            held[i, row, :] = both[i * NF : (i + 1) * NF]
        both = last0[s][:, pl.ds(lane_at, 128)].astype(jnp.float32)
        for pair in range(2):
            held0[pair, row, :] = both[pair * NF : (pair + 1) * NF]
    for i in range(STEP):
        if i % 2 == 0:
            zero = (held0[i // 2] * mask0_ref[i // 2]).T.astype(jnp.bfloat16)
        out_ref[i * 1088 : i * 1088 + 64, :] = zero[i % 2 * 64 : (i % 2 + 1) * 64]
        for tile in range(8):
            at = slice(tile * 128, (tile + 1) * 128)
            block = (held[i, :, at] * mask_ref[0, i : i + 1, at]).T.astype(jnp.bfloat16)
            for half in range(2):
                stop = lax.rem(tile * 2 + half + 15 - y, 16) + 1
                out_ref[pl.ds(pl.multiple_of(i * 1088 + stop * 64, 64), 64), :] = block[half * 64 : (half + 1) * 64]


def finish(y, mask, mask0, outer, inner, pieces, last):
    return pl.pallas_call(
        finish_kernel,
        grid_spec=pltpu.PrefetchScalarGridSpec(
            num_scalar_prefetch=1,
            grid=(32 // STEP,),
            in_specs=[
                pl.BlockSpec((1, STEP, 1024), lambda i, y: (i, 0, 0)),
                pl.BlockSpec((STEP // 2, 1, 128), lambda i, y: (i, 0, 0)),
            ]
            + [
                pl.BlockSpec((4, STEP * NF, 256), lambda i, y: (0, i, 0)),
                pl.BlockSpec((4, 2 * NF, 256), lambda i, y: (0, 16 + i % 4, 0)),
                pl.BlockSpec((4, STEP * NF, 768), lambda i, y: (0, i, 0)),
            ]
            + [pl.BlockSpec((4, STEP * NF, 1024), lambda i, y: (0, i, 0)) for _ in pieces]
            + [pl.BlockSpec((4, 2 * NF, 1024), lambda i, y: (0, 16, 0)) for _ in pieces]
            + [pl.BlockSpec((STEP * NF, 1024), lambda i, y: (i, 0)) for _ in last]
            + [pl.BlockSpec((2 * NF, 1024), lambda i, y: (16, 0)) for _ in last],
            out_specs=pl.BlockSpec((STEP * 1088, 128), lambda i, y: (i, 0)),
            scratch_shapes=[
                pltpu.VMEM((STEP, 128, 1024), jnp.float32),
                pltpu.VMEM((STEP // 2, 128, 128), jnp.float32),
            ],
        ),
        out_shape=jax.ShapeDtypeStruct((34816, 128), jnp.bfloat16),
        compiler_params=pltpu.CompilerParams(vmem_limit_bytes=60 * MB),
        cost_estimate=cost(9.0),
        name="finish",
    )(y, mask, mask0, outer, outer, inner, *pieces, *pieces, *last, *last)


def shift(block, axis, distance):
    size = lax.axis_size(axis)
    return lax.ppermute(block, axis, [(i, (i + distance) % size) for i in range(size)])


def tie(block, after):
    return block if after is None else lax.optimization_barrier((block, after))[0]


def hour_sum(value):
    total = value
    for zh, core in ((0, 1), (1, 0), (1, 1)):
        route = [(i, i ^ (zh * 2 + core)) for i in range(4)]
        total = total + lax.ppermute(value, ("zh", "core"), route)
    return total


def body(samples, gap_starts, valid_counts, owners, pair_mask):
    member = (owners == jnp.arange(HGROUPS, dtype=jnp.int32)[None, :]).astype(jnp.float32)
    group_size = hour_sum(jnp.sum(member, axis=0))
    weight = jnp.sum(member / (HGROUPS * group_size)[None, :], axis=1)
    root = jnp.repeat(jnp.sqrt(weight), 32)[None, :]

    y = lax.axis_index("y").astype(jnp.int32)
    y_arg = y[None]
    mask = jnp.repeat(pair_mask.astype(jnp.float32), 2, axis=2)
    mask0 = mask[:, 0].reshape(16, 1, 128)
    mask = jnp.roll(mask[:, 1:], y + 1, axis=1).reshape(32 // STEP, STEP, 1024)

    spectra = whiten(normalize(samples.reshape(1024, L), gap_starts, valid_counts[:, None]), root)

    def transpose(block, after, name):
        with jax.named_scope(name):
            return lax.all_to_all(tie(block, after), ("zh", "core", "y"), 0, 0, tiled=True)

    def swap(part):
        with jax.named_scope(f"z{part}"):
            return shift(owns[part], "zl", 1)

    p0 = transpose(spectra[0], None, "p0")
    p1 = transpose(spectra[1], p0, "p1")
    x = lax.axis_index("x")

    def exchange(block, name):
        with jax.named_scope(name):
            return lax.all_to_all(block, "y", 0, 0, tiled=True)

    def choose(part):
        with jax.named_scope(f"x{part}"):
            return lax.optimization_barrier([jnp.where(x < d, swapped[part], owns[part]) for d in (1, 2, 3)])

    def gather(part, blocks, before, last):
        with jax.named_scope(f"x{part}"):
            return [shift(tie(block, last if d == 2 else before), "x", -d) for d, block in zip((1, 2, 3), blocks)]

    def do_cross(part, visitors, after):
        return cross(tie(owns[part], after), (*visitors, swapped[part]))

    def send_back(block, after, name):
        sent = [lax.dynamic_index_in_dim(block, (y + s) % 4, 0, keepdims=False) for s in range(4)]
        with jax.named_scope(name):
            return [sent[0]] + [shift(tie(sent[s], after), "y", s) for s in range(1, 4)]

    owns = assemble(p0)
    swapped = [swap(0)]
    chosen = choose(0)
    v0 = gather(0, chosen, None, None)
    a0 = outer(tie(owns[0], chosen), swapped[0])
    ya0 = exchange(tie(a0, p1), "yA0")
    owns += assemble(tie(p1, chosen))
    swapped.append(swap(1))
    p23 = transpose(spectra[2], ya0, "p23")
    owns += assemble(p23)
    swapped += [swap(2), swap(3)]
    c0 = inner(owns[0], v0)
    y0 = exchange(tie(c0, p23), "y0")
    v1 = gather(1, choose(1), None, c0)
    c1 = do_cross(1, v1, (c0, owns[2], owns[3]))
    y1 = exchange(tie(c1, y0), "y1")
    v2 = gather(2, choose(2), v0, c1)
    c2 = do_cross(2, v2, (c1, y0))
    y2 = send_back(c2, None, "y2")
    v3 = gather(3, choose(3), v1, c2)
    c3 = do_cross(3, v3, (c2, y1))
    y3 = send_back(c3, None, "y3")
    return finish(y_arg, mask, mask0, ya0, y0, (y1,), y2 + y3).reshape(32, 17, 32, 2, 128)


def solution(mesh):
    fine = Mesh(mesh.devices.reshape(2, 4, 4, 2, 2), ("zl", "x", "y", "zh", "core"))
    chan, hour = ("zl", "x", "y"), ("zh", "core")
    placed = (
        P(hour, chan, None),
        P(hour, None),
        P(hour),
        P(hour, None),
        P(chan, None, None),
    )
    return jax.shard_map(
        body,
        mesh=fine,
        in_specs=placed,
        out_specs=P(chan, None, None, None, hour),
        check_vma=False,
    )
```
